256 devices in a mesh: aux: 32 (over y, z), row: 8 (over x, core).
Axes of the slice: x: 4, y: 4, z: 8, core: 2. Of those that a mesh axis runs over, the one named last changes fastest.
Arguments:
- three_index: bfloat16 [256, 256, 128, 128], P('aux', 'row'), may hold values from -0.125 to 0.125
- coeffs: bfloat16 [16384, 256], P('aux'), may hold values from -0.375 to 0.375
- pair_owner: int32 [32, 256, 1], P('aux', 'row'), may hold values from 0 to 31; in each aligned block of 32 rows (0 to 31, 32 to 63, ..., all dimensions but the last counted through in order) at most 2 rows name the same one
- pair_tile: int32 [32, 256], P('aux', 'row'), may hold values from 0 to 3
- pair_mblock: int32 [32, 256], P('aux', 'row'), may hold values from 0 to 1
Outputs:
- exchange_matrix: float32 [2048, 2048], P('aux', 'row')
The draws below stay inside these ranges and needn't reach their ends.
Inputs may be any that keep to these rules, and one draw needn't show every extreme that they name: `pair_owner`: among the 32 blocks of one device, no owner is named more than 2 times, and in every draw some device names some owner exactly 2 times; every owner is named somewhere.
All inputs are finite; a program needn't handle non-finite values.
Results may differ from the reference program's by a relative error of at most 0.00079.
Values may be sent and summed in bfloat16 or wider, within the bound.
A program may use at most 64 MiB of HBM per device.

```python
import math
import jax
import jax.numpy as jnp
import numpy as np
from jax import lax

BLK = 128
NOCC = 256
AUX_DEV = 8
ROWS_DEV = 256
LB_DEV = 4
NPAIR = 32
CAP = 2
MB_DEV = 2
NAUX = 256
M = 2048
NL = 16384
N_AUX = 32
N_ROW = 8


def with_ends(array, rng, low, largest):
    spot = [jax.random.randint(jax.random.fold_in(rng, axis), (), 0, length) for axis, length in enumerate(array.shape)]
    widest = array.shape.index(max(array.shape))
    neighbour = spot[:widest] + [(spot[widest] + 1) % array.shape[widest]] + spot[widest + 1:]
    return array.at[tuple(spot)].set(low).at[tuple(neighbour)].set(largest)


def block_levels(key, extent, split, smallest, largest):
    factor_of, own = 1.0, jax.random.fold_in(key, 6)
    for axis_at, blocks in split:
        draws = jnp.exp(jax.random.uniform(jax.random.fold_in(own, axis_at), (blocks,), jnp.float32, smallest / len(split), largest / len(split)))
        factor_of = factor_of * jnp.repeat(draws, extent[axis_at] // blocks).reshape([-1 if axis == axis_at else 1 for axis in range(len(extent))])
    return factor_of


def assign_block(key, own, number, rows, count, top, limit, slope):
    sequence = jax.random.permutation(key, count)
    crowded, usual = load_shares(count, rows * top, limit, slope, True), load_shares(count, rows * top, limit, slope, False)
    places = jnp.arange(count)

    def named(lengths, turn):
        used = int((lengths > 0).sum())
        fixed = max(1, used // 4)
        shifted = fixed + (places - fixed + turn * (used - fixed)) % max(1, count - fixed)
        return jnp.zeros((count,), jnp.int32).at[sequence[jnp.where(places < fixed, places, shifted)]].set(jnp.asarray(lengths, jnp.int32))

    lengths = jnp.where(number % 4 == 0, named(crowded, number // 4), named(usual, number - number // 4 - 1))
    mixed = jax.random.permutation(jax.random.fold_in(own, 3), count)
    donor, receiver = mixed[0:count // 2 * 2:2], mixed[1:count // 2 * 2:2]
    margin = jnp.minimum(lengths[donor] - 1, limit - lengths[receiver]) // 2
    margin = jnp.where((donor == sequence[0]) | (receiver == sequence[0]) | (lengths[receiver] == 0), 0, jnp.maximum(margin, 0))
    shifted = jax.random.randint(jax.random.fold_in(own, 4), (count // 2,), 0, 1 << 20) % (margin + 1)
    lengths = lengths.at[donor].add(-shifted).at[receiver].add(shifted)
    items = jnp.searchsorted(jnp.cumsum(lengths), jnp.arange(rows * top), side="right").astype(jnp.int32)
    grid = items.reshape(top, rows).T
    grid = grid[jax.random.permutation(jax.random.fold_in(own, 1), rows)]
    turn = jax.random.randint(jax.random.fold_in(own, 2), (rows, 1), 0, top)
    return jnp.take_along_axis(grid, (jnp.arange(top)[None, :] + turn) % top, axis=1)


def load_shares(number_of, total, reach, lean, full):
    loads = [(1 << 20) // math.isqrt(rank ** lean) + 1 for rank in range(1, number_of + 1)]
    largest = reach if full else min(reach, max(-(-total // number_of), total * loads[0] // sum(loads)))
    least = 1 if total - largest >= number_of - 1 else 0
    given, rest = [largest] + [least] * (number_of - 1), total - largest - least * (number_of - 1)
    while rest > 0:
        movable = [i for i in range(1, number_of) if given[i] < largest] or [i for i in range(1, number_of) if given[i] < reach]
        mass, remaining = sum([loads[i] for i in movable]), rest
        for i in movable:
            extra = min(reach - given[i], max(1, remaining * loads[i] // mass), rest)
            given[i] = given[i] + extra
            rest = rest - extra
    return np.array(given)


def noise(own_key, extent, spread, bound, shards=(), dtype=jnp.bfloat16):
    entries = spread * jax.random.normal(own_key, extent, jnp.float32)
    if shards:
        entries = entries * block_levels(own_key, extent, shards, -0.22, 0.18)
    return jnp.clip(entries, -bound, bound).astype(dtype)


def setup_inputs(seed: int = 0) -> dict:
    seeds = jax.random.split(jax.random.key(seed), 6)
    three_index = noise(seeds[0], (NAUX, N_ROW * NPAIR, BLK, BLK), (BLK * NPAIR // MB_DEV) ** -0.5, 0.125, ((0, 32), (1, 8)))
    coeffs = noise(seeds[1], (NL, NOCC), NOCC ** -0.5, 0.375, ((0, 32),))
    pair_owner_keys = jax.random.split(jax.random.fold_in(seeds[2], 1), N_AUX * (N_ROW * NPAIR) // NPAIR)
    pair_owner_turns = jax.random.permutation(jax.random.fold_in(seeds[2], 3), N_AUX * (N_ROW * NPAIR) // NPAIR)
    pair_owner = jax.vmap(lambda own, number: assign_block(jax.random.fold_in(seeds[2], 2), own, number, NPAIR, N_AUX, 1, CAP, 2))(pair_owner_keys, pair_owner_turns).reshape((N_AUX, N_ROW * NPAIR, 1))
    pair_tile = with_ends(jax.random.randint(seeds[3], (N_AUX, N_ROW * NPAIR), 0, LB_DEV), jax.random.fold_in(seeds[3], 1), 0, LB_DEV - 1).astype(jnp.int32)
    pair_mblock = with_ends(jax.random.randint(seeds[4], (N_AUX, N_ROW * NPAIR), 0, MB_DEV), jax.random.fold_in(seeds[4], 1), 0, MB_DEV - 1).astype(jnp.int32)
    return dict(three_index=three_index, coeffs=coeffs, pair_owner=pair_owner, pair_tile=pair_tile, pair_mblock=pair_mblock)


def reference(three_index, coeffs, pair_owner, pair_tile, pair_mblock):
    row_blocks = ROWS_DEV // BLK
    coeff_blocks = coeffs.reshape(N_AUX * LB_DEV, BLK, NOCC)
    lblock = (pair_owner[:, :, 0] * LB_DEV + pair_tile).astype(jnp.int32)
    slabs = three_index.reshape(N_AUX, AUX_DEV, N_ROW, NPAIR, BLK, BLK)
    lblock = lblock.reshape(N_AUX, N_ROW, NPAIR)
    row_block = pair_mblock.reshape(N_AUX, N_ROW, NPAIR)

    def shard(accumulated, shard_index):
        slab_here = lax.dynamic_index_in_dim(slabs, shard_index, 0, keepdims=False)
        block_here = lax.dynamic_index_in_dim(lblock, shard_index, 0, keepdims=False)
        rows_here = lax.dynamic_index_in_dim(row_block, shard_index, 0, keepdims=False)
        coeff_here = coeff_blocks[block_here]
        products = jnp.einsum('prkml,rkli->prkmi', slab_here.astype(jnp.float32), coeff_here.astype(jnp.float32), precision=lax.Precision.HIGHEST)
        selector = (rows_here[:, :, None] == jnp.arange(row_blocks)[None, None, :]).astype(jnp.float32)
        half_transform = jnp.einsum('rkb,prkmi->prbmi', selector, products, precision=lax.Precision.HIGHEST)
        half_transform = half_transform.reshape(AUX_DEV, M, NOCC).astype(jnp.bfloat16)
        flattened = half_transform.astype(jnp.float32).transpose(1, 0, 2).reshape(M, AUX_DEV * NOCC)
        return accumulated + jnp.dot(flattened, flattened.T, precision=lax.Precision.HIGHEST), None

    exchange_matrix, _ = lax.scan(shard, jnp.zeros((M, M), jnp.float32), jnp.arange(N_AUX))
    return exchange_matrix
```

```python
import functools

import jax
import jax.numpy as jnp
from jax import lax
from jax.experimental import pallas as pl
from jax.experimental.pallas import tpu as pltpu
from jax.sharding import PartitionSpec as P

MESH = pl.DeviceIdType.MESH
NX, NY, NZ = 4, 4, 8
BLK = 128
F32, BF16 = jnp.float32, jnp.bfloat16


def broadcast_tree():
    parent = {}
    for dz in (1, 2, 3, 4):
        parent[0, dz] = (0, dz - 1)
    for dz in (-1, -2, -3):
        parent[0, dz] = (0, dz + 1)
    for dz in range(-3, 5):
        parent[1, dz] = (0, dz)
        parent[-1, dz] = (0, dz)
    parent[1, 4] = (1, 3)
    parent[2, 0] = (1, 0)
    for dz in (1, 2, 3):
        parent[2, dz] = (2, dz - 1)
    for dz in (-1, -2, -3, -4):
        parent[2, dz] = (2, dz + 1)
    return parent


PARENT = broadcast_tree()
ARRIVALS = [
    (1, 0), (-1, 0), (0, 1), (0, -1), (2, 0), (-1, 1), (0, 2), (0, -2), (1, 1), (-1, -1), (2, 1), (2, -1),
    (1, -1), (-1, 2), (0, 3), (0, -3), (1, 2), (-1, -2), (2, 2), (2, -2), (1, -2), (-1, 3), (0, 4), (1, 3),
    (2, -3), (-1, -3), (2, 3), (1, -3), (-1, 4), (1, 4), (2, -4),
]
SLOT = {offset: i for i, offset in enumerate(ARRIVALS)}


def height(offset):
    return 1 + max([height(o) for o in PARENT if PARENT[o] == offset], default=0)


CHILDREN = {
    offset: sorted([o for o in PARENT if PARENT[o] == offset], key=lambda o: -height(o))
    for offset in [(0, 0)] + ARRIVALS
}


def kernel(
    owner_ref, tile_ref, mblock_ref, coef_ref, t_hbm, out_ref,
    t_buf, c_buf0, c_buf1, rhs, acc, h_buf, g_buf, z_out, z_in, y_sum, y_in,
    t_sem, c_recv, c_send, cf_recv, cf_send, h_recv, h_send, hf_recv, hf_send, z_recv, z_send, y_recv, y_send,
):
    a, r = lax.axis_index("aux"), lax.axis_index("row")
    y, z = a // NZ, lax.rem(a, NZ)
    x, c = r // 2, lax.rem(r, 2)
    sign = 1 - 2 * c

    def at(dx=0, dy=0, dz=0, flip=0):
        return {
            "aux": lax.rem(y + dy + NY, NY) * NZ + lax.rem(z + dz + NZ, NZ),
            "row": lax.rem(x + dx + NX, NX) * 2 + lax.rem(c + flip, 2),
        }

    def copy(src, dst, send, recv, device):
        return pltpu.make_async_remote_copy(
            src_ref=src, dst_ref=dst, send_sem=send, recv_sem=recv, device_id=device, device_id_type=MESH
        )

    c_bufs = (c_buf0, c_buf1)
    sibling = at(flip=1)
    t_copy = pltpu.make_async_copy(t_hbm, t_buf, t_sem)
    t_copy.start()
    partners = [sibling]
    partners += [at(dx=e) for e in range(1, NX)]
    partners += [at(dy=e) for e in range(1, NY)]
    partners += [at(dz=e) for e in range(1, NZ)]
    barrier = pltpu.get_barrier_semaphore()
    for device in partners:
        pl.semaphore_signal(barrier, inc=1, device_id=device, device_id_type=MESH)
    for ch in range(2):
        for t in range(4):
            c_bufs[ch][a * 4 + t] = coef_ref[t * BLK:(t + 1) * BLK, ch * BLK:(ch + 1) * BLK]
    pl.semaphore_wait(barrier, len(partners))

    def relay(ch, offset):
        dy, dz = offset
        origin = lax.rem(y - sign * dy + NY, NY) * NZ + lax.rem(z - sign * dz + NZ, NZ)
        piece = c_bufs[ch].at[pl.ds(origin * 4 + 2 * c, 2)]
        if offset != (0, 0):
            copy(piece, piece, c_send.at[ch], c_recv.at[ch, SLOT[offset]], sibling).wait_recv()
        for child in CHILDREN[offset]:
            to = at(dy=sign * (child[0] - dy), dz=sign * (child[1] - dz))
            copy(piece, piece, c_send.at[ch], c_recv.at[ch, SLOT[child]], to).start()
        if offset != (0, 0):
            copy(piece, piece, cf_send.at[ch], cf_recv.at[ch], sibling).start()

    carried = c_buf0.at[pl.ds(0, 2 * len(ARRIVALS))]

    def wait_flipped(ch):
        copy(carried, carried, cf_send.at[ch], cf_recv.at[ch], sibling).wait_recv()

    def build_rhs(ch):
        for k in range(32):
            block = c_bufs[ch][owner_ref[k] * 4 + tile_ref[k]]
            zero = jnp.zeros_like(block)
            for b in range(2):
                rhs[k * BLK:(k + 1) * BLK, b * BLK:(b + 1) * BLK] = jnp.where(mblock_ref[k] == b, block, zero)

    def half_dot(g):
        lhs = jnp.concatenate([t_buf[:, 4 * g + j].reshape(8 * BLK, BLK) for j in range(4)], axis=1)
        product = jnp.dot(lhs, rhs[g * 512:(g + 1) * 512, :], preferred_element_type=F32)
        if g == 0:
            acc[...] = product
        else:
            acc[...] += product

    def store_half(ch):
        for p in range(8):
            for b in range(2):
                h_buf[ch, 0, c, b * BLK:(b + 1) * BLK, p * BLK:(p + 1) * BLK] = acc[
                    p * BLK:(p + 1) * BLK, b * BLK:(b + 1) * BLK
                ].astype(BF16)

    def send_half(ch, e):
        d = (NX - e) % NX
        return copy(h_buf.at[ch, 0, c], h_buf.at[ch, d, c], h_send.at[ch, e], h_recv.at[ch, d], at(dx=e))

    def flip_half(ch, d):
        ref = h_buf.at[ch, d, c]
        return copy(ref, ref, hf_send.at[ch, d], hf_recv.at[ch, d], sibling)

    def gram(d):
        for src in range(2):
            total = None
            for ch in range(2):
                part = lax.dot_general(
                    h_buf[ch, d, src], h_buf[ch, 0, c], (((1,), (1,)), ((), ())), preferred_element_type=F32
                )
                total = part if total is None else total + part
            g_buf[src * 256:(src + 1) * 256, :] = total
            z_out[d, src * 256:(src + 1) * 256, :] = total.astype(BF16)
        y_sum[d] = g_buf[pl.ds(pl.multiple_of(z * 64, 64), 64), :]

    def z_copy(d, e):
        rows = pl.ds(pl.multiple_of(lax.rem(z + e, NZ) * 64, 64), 64)
        return copy(z_out.at[d, rows], z_in.at[d, e - 1], z_send.at[d], z_recv.at[d], at(dz=e))

    def z_start(d):
        for e in (4, 3, 5, 2, 6, 1, 7):
            z_copy(d, e).start()

    def y_copy(d):
        plane = lax.rem(x + d, NX)
        slot = lax.rem(y - plane + 2 * NY - 1, NY)
        to = {"aux": plane * NZ + z, "row": r}
        return plane, copy(y_sum.at[d], y_in.at[slot], y_send.at[d], y_recv.at[slot], to)

    def z_finish(d):
        copy(z_in.at[d], z_in.at[d], z_send.at[d], z_recv.at[d], sibling).wait_recv()
        total = y_sum[d]
        for e in range(NZ - 1):
            total = total + z_in[d, e].astype(F32)
        y_sum[d] = total
        plane, send = y_copy(d)
        pl.when(plane != y)(send.start)

    relay(0, (0, 0))
    for i, offset in enumerate(ARRIVALS):
        relay(0, offset)
        if i == 15:
            relay(1, (0, 0))
    wait_flipped(0)
    t_copy.wait()
    build_rhs(0)
    later = list(ARRIVALS)
    for g in range(8):
        half_dot(g)
        relay(1, later.pop(0))
    store_half(0)
    flip_half(0, 0).start()
    send_half(0, 1).start()
    send_half(0, 3).start()
    for offset in later:
        relay(1, offset)
    wait_flipped(1)
    build_rhs(1)
    for g in range(8):
        half_dot(g)
    store_half(1)
    flip_half(1, 0).start()
    send_half(1, 1).start()
    send_half(1, 3).start()
    for d in (1, 3):
        flip = flip_half(0, d)
        send_half(0, NX - d).wait_recv()
        flip.start()
    flip_half(0, 0).wait_recv()
    flip_half(1, 0).wait_recv()
    gram(0)
    z_start(0)
    send_half(0, 2).start()
    send_half(1, 2).start()
    z_finish(0)
    for d in (1, 3):
        send_half(1, NX - d).wait_recv()
        flip_half(1, d).start()
    for d in (1, 3):
        flip_half(0, d).wait_recv()
        flip_half(1, d).wait_recv()
        gram(d)
        z_start(d)
    for d in (1, 3):
        z_finish(d)
    for ch in range(2):
        send_half(ch, 2).wait_recv()
        flip_half(ch, 2).start()
    for ch in range(2):
        flip_half(ch, 2).wait_recv()
    gram(2)
    z_start(2)
    z_finish(2)
    for slot in range(NY - 1):
        copy(y_in.at[slot], y_in.at[slot], y_send.at[0], y_recv.at[slot], sibling).wait_recv()
    out_ref[...] = y_sum[lax.rem(y - x + NY, NY)] + y_in[0] + y_in[1] + y_in[2]

    for ch in range(2):
        copy(carried, carried, c_send.at[ch], c_recv.at[ch, 0], sibling).wait_send()
        copy(carried, carried, cf_send.at[ch], cf_recv.at[ch], sibling).wait_send()
        for e in range(1, NX):
            send_half(ch, e).wait_send()
        for d in range(NX):
            flip_half(ch, d).wait_send()
    for d in range(NX):
        copy(z_in.at[d], z_in.at[d], z_send.at[d], z_recv.at[d], sibling).wait_send()
        plane, send = y_copy(d)
        pl.when(plane != y)(send.wait_send)


def shards(three_index, coeffs, pair_owner, pair_tile, pair_mblock):
    smem, vmem = pl.BlockSpec(memory_space=pltpu.SMEM), pl.BlockSpec(memory_space=pltpu.VMEM)
    dma = pltpu.SemaphoreType.DMA
    return pl.pallas_call(
        kernel,
        out_shape=jax.ShapeDtypeStruct((64, 256), F32),
        in_specs=[smem, smem, smem, vmem, pl.BlockSpec(memory_space=pl.ANY)],
        out_specs=vmem,
        scratch_shapes=[
            pltpu.VMEM((8, 32, BLK, BLK), BF16),
            pltpu.VMEM((128, BLK, BLK), BF16),
            pltpu.VMEM((128, BLK, BLK), BF16),
            pltpu.VMEM((32 * BLK, 256), BF16),
            pltpu.VMEM((8 * BLK, 256), F32),
            pltpu.VMEM((2, 4, 2, 256, 1024), BF16),
            pltpu.VMEM((512, 256), F32),
            pltpu.VMEM((4, 512, 256), BF16),
            pltpu.VMEM((4, 7, 64, 256), BF16),
            pltpu.VMEM((4, 64, 256), F32),
            pltpu.VMEM((4, 64, 256), F32),
            dma, dma((2, 31)), dma((2,)), dma((2,)), dma((2,)),
            dma((2, 4)), dma((2, 4)), dma((2, 4)), dma((2, 4)),
            dma((4,)), dma((4,)), dma((4,)), dma((4,)),
        ],
        compiler_params=pltpu.CompilerParams(
            collective_id=0, has_side_effects=True, vmem_limit_bytes=56 * 1024 * 1024
        ),
        name="exchange",
    )(pair_owner.reshape(32), pair_tile.reshape(32), pair_mblock.reshape(32), coeffs, three_index)


def solution(mesh):
    placed = (
        P("aux", "row", None, None),
        P("aux", None),
        P("aux", "row", None),
        P("aux", "row"),
        P("aux", "row"),
    )
    return jax.shard_map(
        shards, mesh=mesh, in_specs=placed, out_specs=P("aux", "row"), check_vma=False
    )
```

```python
import jax
import jax.numpy as jnp
from jax import lax
from jax.experimental import pallas as pl
from jax.experimental.pallas import tpu as pltpu
from jax.sharding import PartitionSpec as P

MESH = pl.DeviceIdType.MESH
NX, NY, NZ = 4, 4, 8
BLK = 128
F32, BF16 = jnp.float32, jnp.bfloat16


TREE = (
    (0, 0, 0, ((0, 2, 0), (0, 6, 0), (1, 0, 0), (0, 7, 0),)),
    (1, 0, 0, ((3, 0, 0),)),
    (0, 1, 0, ((1, 1, 0), (2, 0, 0), (3, 0, 1),)),
    (1, 3, 0, ((3, 7, 0), (3, 3, 0), (1, 0, 1), (2, 0, 0),)),
    (0, 0, 2, ((3, 2, 0),)),
    (0, 0, 6, ((0, 4, 0), (0, 5, 0), (1, 6, 0), (3, 6, 0),)),
    (0, 0, 7, ((1, 7, 0),)),
    (0, 1, 1, ((3, 1, -1), (0, 1, 0),)),
    (0, 2, 0, ((2, 7, 0),)),
    (0, 3, 0, ()),
    (1, 3, 7, ((0, 7, 0), (1, 7, -1), (3, 5, 0), (2, 7, 0),)),
    (1, 2, 0, ()),
    (1, 1, 0, ((1, 1, 0),)),
    (0, 3, 2, ((3, 3, 0), (1, 2, 1), (2, 2, 0),)),
    (0, 1, 6, ((2, 6, 0),)),
    (0, 3, 6, ((3, 5, 0),)),
    (0, 1, 7, ((3, 7, 1),)),
    (0, 3, 1, ((2, 1, 0),)),
    (0, 0, 4, ((1, 4, 0), (0, 3, 0),)),
    (0, 0, 1, ()),
    (0, 0, 5, ((1, 5, 0), (2, 5, 0),)),
    (1, 0, 7, ((0, 1, 0),)),
    (1, 1, 7, ((1, 6, 0),)),
    (1, 3, 3, ((1, 3, -1),)),
    (1, 1, 1, ()),
    (0, 1, 2, ()),
    (1, 2, 7, ((2, 1, 0),)),
    (0, 2, 7, ()),
    (0, 2, 6, ()),
    (0, 3, 3, ((1, 3, -1), (2, 3, 0),)),
    (0, 3, 7, ()),
    (0, 2, 2, ()),
    (0, 1, 4, ((2, 4, 0), (3, 4, 1),)),
    (0, 2, 1, ()),
    (1, 1, 3, ((1, 2, 0), (1, 4, 0), (0, 3, 0), (2, 3, 0),)),
    (0, 1, 5, ()),
    (1, 3, 5, ((0, 5, 0), (2, 5, 0), (3, 4, 0),)),
    (0, 3, 5, ()),
    (1, 0, 1, ((0, 2, 0), (3, 1, 0),)),
    (0, 1, 3, ()),
    (0, 2, 5, ()),
    (0, 3, 4, ()),
    (0, 2, 3, ()),
    (0, 0, 3, ()),
    (0, 2, 4, ()),
    (1, 0, 3, ()),
    (1, 1, 6, ((2, 6, 0), (3, 6, -1),)),
    (1, 2, 3, ()),
    (1, 2, 1, ()),
    (1, 1, 4, ((0, 4, 0), (1, 5, 0),)),
    (1, 2, 5, ((2, 4, 0),)),
    (1, 1, 2, ((2, 2, 0),)),
    (1, 0, 5, ((0, 6, 0),)),
    (1, 0, 2, ((3, 2, 0),)),
    (1, 3, 1, ()),
    (1, 3, 4, ()),
    (1, 2, 6, ()),
    (1, 3, 6, ()),
    (1, 0, 4, ()),
    (1, 1, 5, ()),
    (1, 2, 4, ()),
    (1, 2, 2, ()),
    (1, 3, 2, ()),
    (1, 0, 6, ()),
)

SLOT = {entry[:3]: i for i, entry in enumerate(TREE)}


def kernel(
    owner_ref, tile_ref, mblock_ref, coef_ref, t_hbm, out_ref,
    t_buf, c_buf0, c_buf1, rhs, acc, h_buf, g_buf, z_out, z_in, y_sum, y_in,
    t_sem, c_recv, c_send, cf_recv, cf_send, h_recv, h_send, f_recv, f_send, hf_recv, hf_send, z_recv, z_send, y_recv, y_send,
):
    a, r = lax.axis_index("aux"), lax.axis_index("row")
    y, z = a // NZ, lax.rem(a, NZ)
    x, c = r // 2, lax.rem(r, 2)
    sign_z = 1 - 2 * c
    sign_y = sign_z * (1 - 2 * lax.rem(x, 2))

    def at(dx=0, dy=0, dz=0, flip=0):
        return {
            "aux": lax.rem(y + dy + NY, NY) * NZ + lax.rem(z + dz + NZ, NZ),
            "row": lax.rem(x + dx + NX, NX) * 2 + lax.rem(c + flip, 2),
        }

    def copy(src, dst, send, recv, device):
        return pltpu.make_async_remote_copy(
            src_ref=src, dst_ref=dst, send_sem=send, recv_sem=recv, device_id=device, device_id_type=MESH
        )

    c_bufs = (c_buf0, c_buf1)
    sibling = at(flip=1)
    t_copy = pltpu.make_async_copy(t_hbm, t_buf, t_sem)
    t_copy.start()
    partners = [sibling]
    partners += [at(dx=e) for e in (1, 3)]
    partners += [at(dy=e) for e in range(1, NY)]
    partners += [at(dz=e) for e in range(1, NZ)]
    barrier = pltpu.get_barrier_semaphore()
    for device in partners:
        pl.semaphore_signal(barrier, inc=1, device_id=device, device_id_type=MESH)
    for ch in range(2):
        for t in range(4):
            c_bufs[ch][a * 4 + t] = coef_ref[t * BLK:(t + 1) * BLK, ch * BLK:(ch + 1) * BLK]
    pl.semaphore_wait(barrier, len(partners))

    def relay(entry):
        ch, dy, dz, children = entry
        origin = lax.rem(y - sign_y * dy + NY, NY) * NZ + lax.rem(z - sign_z * dz + NZ, NZ)
        piece = c_bufs[ch].at[pl.ds(origin * 4 + 2 * c, 2)]
        if dy or dz:
            copy(piece, piece, c_send.at[ch], c_recv.at[SLOT[ch, dy, dz]], sibling).wait_recv()
        for child_dy, child_dz, dx in children:
            to = at(dx=dx) if dx else at(dy=sign_y * (child_dy - dy), dz=sign_z * (child_dz - dz))
            copy(piece, piece, c_send.at[ch], c_recv.at[SLOT[ch, child_dy, child_dz]], to).start()
        if dy or dz:
            copy(piece, piece, cf_send.at[ch], cf_recv.at[ch], sibling).start()

    carried = c_buf0.at[pl.ds(0, 62)]

    def wait_flipped(ch):
        copy(carried, carried, cf_send.at[ch], cf_recv.at[ch], sibling).wait_recv()

    def build_rhs(ch):
        for k in range(32):
            block = c_bufs[ch][owner_ref[k] * 4 + tile_ref[k]]
            zero = jnp.zeros_like(block)
            for b in range(2):
                rhs[k * BLK:(k + 1) * BLK, b * BLK:(b + 1) * BLK] = jnp.where(mblock_ref[k] == b, block, zero)

    def half_dot(g):
        lhs = jnp.concatenate([t_buf[:, 4 * g + j].reshape(8 * BLK, BLK) for j in range(4)], axis=1)
        product = jnp.dot(lhs, rhs[g * 512:(g + 1) * 512, :], preferred_element_type=F32)
        if g == 0:
            acc[...] = product
        else:
            acc[...] += product

    def store_half(ch):
        for p in range(8):
            for b in range(2):
                h_buf[ch, 0, c, b * BLK:(b + 1) * BLK, p * BLK:(p + 1) * BLK] = acc[
                    p * BLK:(p + 1) * BLK, b * BLK:(b + 1) * BLK
                ].astype(BF16)

    def send_half(ch, e):
        d = (NX - e) % NX
        return copy(h_buf.at[ch, 0, c], h_buf.at[ch, d, c], h_send.at[ch, e], h_recv.at[ch, d], at(dx=e))

    def pass_half(ch, e):
        d, rows = (NX - e) % NX, pl.ds(0 if e == 1 else BLK, BLK)
        return copy(
            h_buf.at[ch, d, c, rows], h_buf.at[ch, 2, c, rows], f_send.at[ch, e], f_recv.at[ch, e], at(dx=e)
        )

    def flip_half(ch, d):
        ref = h_buf.at[ch, d, c]
        return copy(ref, ref, hf_send.at[ch, d], hf_recv.at[ch, d], sibling)

    def gram(d):
        for src in range(2):
            total = None
            for ch in range(2):
                part = lax.dot_general(
                    h_buf[ch, d, src], h_buf[ch, 0, c], (((1,), (1,)), ((), ())), preferred_element_type=F32
                )
                total = part if total is None else total + part
            g_buf[src * 256:(src + 1) * 256, :] = total
            z_out[d, src * 256:(src + 1) * 256, :] = total.astype(BF16)
        y_sum[d] = g_buf[pl.ds(pl.multiple_of(z * 64, 64), 64), :]

    def z_copy(d, e):
        rows = pl.ds(pl.multiple_of(lax.rem(z + e, NZ) * 64, 64), 64)
        return copy(z_out.at[d, rows], z_in.at[d, e - 1], z_send.at[d], z_recv.at[d], at(dz=e))

    def z_start(d):
        for e in (4, 3, 5, 2, 6, 1, 7):
            z_copy(d, e).start()

    def y_copy(d):
        plane = lax.rem(x + d, NX)
        slot = lax.rem(y - plane + 2 * NY - 1, NY)
        to = {"aux": plane * NZ + z, "row": r}
        return plane, copy(y_sum.at[d], y_in.at[slot], y_send.at[d], y_recv.at[slot], to)

    def z_finish(d):
        copy(z_in.at[d], z_in.at[d], z_send.at[d], z_recv.at[d], sibling).wait_recv()
        total = y_sum[d]
        for e in range(NZ - 1):
            total = total + z_in[d, e].astype(F32)
        y_sum[d] = total
        plane, send = y_copy(d)
        pl.when(plane != y)(send.start)

    done = max(i for i, entry in enumerate(TREE) if entry[0] == 0) + 1
    for entry in TREE[:done]:
        relay(entry)
    later = list(TREE[done:])
    wait_flipped(0)
    t_copy.wait()
    build_rhs(0)
    for g in range(8):
        half_dot(g)
        if later:
            relay(later.pop(0))
    store_half(0)
    send_half(0, 1).start()
    send_half(0, 3).start()
    flip_half(0, 0).start()
    for entry in later:
        relay(entry)
    wait_flipped(1)
    build_rhs(1)
    for g in range(8):
        half_dot(g)
    store_half(1)
    send_half(1, 1).start()
    send_half(1, 3).start()
    flip_half(1, 0).start()
    for ch in range(2):
        for d in (1, 3):
            send_half(ch, NX - d).wait_recv()
            pass_half(ch, NX - d).start()
            flip_half(ch, d).start()
        if ch == 0:
            for src in range(2):
                flip_half(src, 0).wait_recv()
            gram(0)
            z_start(0)
    z_finish(0)
    for d in (1, 3):
        flip_half(0, d).wait_recv()
        flip_half(1, d).wait_recv()
        gram(d)
        z_start(d)
    for d in (1, 3):
        z_finish(d)
    for ch in range(2):
        for e in (1, 3):
            pass_half(ch, e).wait_recv()
        flip_half(ch, 2).start()
    for ch in range(2):
        flip_half(ch, 2).wait_recv()
    gram(2)
    z_start(2)
    z_finish(2)
    for slot in range(NY - 1):
        copy(y_in.at[slot], y_in.at[slot], y_send.at[0], y_recv.at[slot], sibling).wait_recv()
    out_ref[...] = y_sum[lax.rem(y - x + NY, NY)] + y_in[0] + y_in[1] + y_in[2]

    for ch in range(2):
        copy(carried, carried, c_send.at[ch], c_recv.at[0], sibling).wait_send()
        copy(carried, carried, cf_send.at[ch], cf_recv.at[ch], sibling).wait_send()
        for e in (1, 3):
            send_half(ch, e).wait_send()
            pass_half(ch, e).wait_send()
        for d in range(NX):
            flip_half(ch, d).wait_send()
    for d in range(NX):
        copy(z_in.at[d], z_in.at[d], z_send.at[d], z_recv.at[d], sibling).wait_send()
        plane, send = y_copy(d)
        pl.when(plane != y)(send.wait_send)


def shards(three_index, coeffs, pair_owner, pair_tile, pair_mblock):
    smem, vmem = pl.BlockSpec(memory_space=pltpu.SMEM), pl.BlockSpec(memory_space=pltpu.VMEM)
    dma = pltpu.SemaphoreType.DMA
    return pl.pallas_call(
        kernel,
        out_shape=jax.ShapeDtypeStruct((64, 256), F32),
        in_specs=[smem, smem, smem, vmem, pl.BlockSpec(memory_space=pl.ANY)],
        out_specs=vmem,
        scratch_shapes=[
            pltpu.VMEM((8, 32, BLK, BLK), BF16),
            pltpu.VMEM((128, BLK, BLK), BF16),
            pltpu.VMEM((128, BLK, BLK), BF16),
            pltpu.VMEM((32 * BLK, 256), BF16),
            pltpu.VMEM((8 * BLK, 256), F32),
            pltpu.VMEM((2, 4, 2, 256, 1024), BF16),
            pltpu.VMEM((512, 256), F32),
            pltpu.VMEM((4, 512, 256), BF16),
            pltpu.VMEM((4, 7, 64, 256), BF16),
            pltpu.VMEM((4, 64, 256), F32),
            pltpu.VMEM((4, 64, 256), F32),
            dma, dma((64,)), dma((2,)), dma((2,)), dma((2,)),
            dma((2, 4)), dma((2, 4)), dma((2, 4)), dma((2, 4)), dma((2, 4)), dma((2, 4)),
            dma((4,)), dma((4,)), dma((4,)), dma((4,)),
        ],
        compiler_params=pltpu.CompilerParams(
            collective_id=0, has_side_effects=True, vmem_limit_bytes=56 * 1024 * 1024
        ),
        name="exchange",
    )(pair_owner.reshape(32), pair_tile.reshape(32), pair_mblock.reshape(32), coeffs, three_index)


def solution(mesh):
    placed = (
        P("aux", "row", None, None),
        P("aux", None),
        P("aux", "row", None),
        P("aux", "row"),
        P("aux", "row"),
    )
    return jax.shard_map(
        shards, mesh=mesh, in_specs=placed, out_specs=P("aux", "row"), check_vma=False
    )
```

```python
import jax
import jax.numpy as jnp
from jax import lax
from jax.experimental import pallas as pl
from jax.experimental.pallas import tpu as pltpu
from jax.sharding import PartitionSpec as P

MESH = pl.DeviceIdType.MESH
NX, NY, NZ = 4, 4, 8
BLK = 128
F32, BF16 = jnp.float32, jnp.bfloat16


TREE = (
    (0, 0, 0, ((0, 2, 0), (0, 6, 0), (1, 0, 0), (0, 7, 0),)),
    (1, 0, 0, ((3, 0, 0),)),
    (0, 1, 0, ((1, 1, 0), (2, 0, 0), (3, 0, 1),)),
    (1, 3, 0, ((3, 7, 0), (3, 3, 0), (1, 0, 1), (2, 0, 0),)),
    (0, 0, 2, ((3, 2, 0),)),
    (0, 0, 6, ((0, 4, 0), (0, 5, 0), (1, 6, 0), (3, 6, 0),)),
    (0, 0, 7, ((1, 7, 0),)),
    (0, 1, 1, ((3, 1, -1), (0, 1, 0),)),
    (0, 2, 0, ((2, 7, 0),)),
    (0, 3, 0, ()),
    (1, 3, 7, ((0, 7, 0), (1, 7, -1), (3, 5, 0), (2, 7, 0),)),
    (1, 2, 0, ()),
    (1, 1, 0, ((1, 1, 0),)),
    (0, 3, 2, ((3, 3, 0), (1, 2, 1), (2, 2, 0),)),
    (0, 1, 6, ((2, 6, 0),)),
    (0, 3, 6, ((3, 5, 0),)),
    (0, 1, 7, ((3, 7, 1),)),
    (0, 3, 1, ((2, 1, 0),)),
    (0, 0, 4, ((1, 4, 0), (0, 3, 0),)),
    (0, 0, 1, ()),
    (0, 0, 5, ((1, 5, 0), (2, 5, 0),)),
    (1, 0, 7, ((0, 1, 0),)),
    (1, 1, 7, ((1, 6, 0),)),
    (1, 3, 3, ((1, 3, -1),)),
    (1, 1, 1, ()),
    (0, 1, 2, ()),
    (1, 2, 7, ((2, 1, 0),)),
    (0, 2, 7, ()),
    (0, 2, 6, ()),
    (0, 3, 3, ((1, 3, -1), (2, 3, 0),)),
    (0, 3, 7, ()),
    (0, 2, 2, ()),
    (0, 1, 4, ((2, 4, 0), (3, 4, 1),)),
    (0, 2, 1, ()),
    (1, 1, 3, ((1, 2, 0), (1, 4, 0), (0, 3, 0), (2, 3, 0),)),
    (0, 1, 5, ()),
    (1, 3, 5, ((0, 5, 0), (2, 5, 0), (3, 4, 0),)),
    (0, 3, 5, ()),
    (1, 0, 1, ((0, 2, 0), (3, 1, 0),)),
    (0, 1, 3, ()),
    (0, 2, 5, ()),
    (0, 3, 4, ()),
    (0, 2, 3, ()),
    (0, 0, 3, ()),
    (0, 2, 4, ()),
    (1, 0, 3, ()),
    (1, 1, 6, ((2, 6, 0), (3, 6, -1),)),
    (1, 2, 3, ()),
    (1, 2, 1, ()),
    (1, 1, 4, ((0, 4, 0), (1, 5, 0),)),
    (1, 2, 5, ((2, 4, 0),)),
    (1, 1, 2, ((2, 2, 0),)),
    (1, 0, 5, ((0, 6, 0),)),
    (1, 0, 2, ((3, 2, 0),)),
    (1, 3, 1, ()),
    (1, 3, 4, ()),
    (1, 2, 6, ()),
    (1, 3, 6, ()),
    (1, 0, 4, ()),
    (1, 1, 5, ()),
    (1, 2, 4, ()),
    (1, 2, 2, ()),
    (1, 3, 2, ()),
    (1, 0, 6, ()),
)

SLOT = {entry[:3]: i for i, entry in enumerate(TREE)}


def kernel(
    owner_ref, tile_ref, mblock_ref, coef_ref, t_hbm, out_ref,
    t_buf, c_buf0, c_buf1, rhs, acc, h_own, h_nbr, h_far, g_buf, z_out, z_in, y_sum, y_in, x_pad, x_out, x_in,
    t_sem, c_recv, c_send, cf_recv, cf_send, n_recv, n_send, f_recv, f_send, of_recv, of_send, nf_recv, nf_send,
    ff_recv, ff_send, z_recv, z_send, y_recv, y_send, x_recv, x_send,
):
    a, r = lax.axis_index("aux"), lax.axis_index("row")
    y, z = a // NZ, lax.rem(a, NZ)
    x, c = r // 2, lax.rem(r, 2)
    sign_z = 1 - 2 * c
    sign_y = sign_z * (1 - 2 * lax.rem(x, 2))

    def at(dx=0, dy=0, dz=0, flip=0):
        return {
            "aux": lax.rem(y + dy + NY, NY) * NZ + lax.rem(z + dz + NZ, NZ),
            "row": lax.rem(x + dx + NX, NX) * 2 + lax.rem(c + flip, 2),
        }

    def copy(src, dst, send, recv, device):
        return pltpu.make_async_remote_copy(
            src_ref=src, dst_ref=dst, send_sem=send, recv_sem=recv, device_id=device, device_id_type=MESH
        )

    c_bufs = (c_buf0, c_buf1)
    sibling = at(flip=1)
    t_copy = pltpu.make_async_copy(t_hbm, t_buf, t_sem)
    t_copy.start()
    partners = [sibling]
    partners += [at(dx=e) for e in (1, 3)]
    partners += [at(dy=e) for e in range(1, NY)]
    partners += [at(dz=e) for e in range(1, NZ)]
    mirrors = [{"aux": x * NZ + 4 * c + t, "row": y * 2 + z // 4} for t in range(4)]
    barrier = pltpu.get_barrier_semaphore()
    for device in partners:
        pl.semaphore_signal(barrier, inc=1, device_id=device, device_id_type=MESH)

    @pl.when(x != y)
    def _():
        for device in mirrors:
            pl.semaphore_signal(barrier, inc=1, device_id=device, device_id_type=MESH)

    for ch in range(2):
        for t in range(4):
            c_bufs[ch][a * 4 + t] = coef_ref[t * BLK:(t + 1) * BLK, ch * BLK:(ch + 1) * BLK]

    @pl.when(x == y)
    def _():
        pl.semaphore_wait(barrier, len(partners))

    @pl.when(x != y)
    def _():
        pl.semaphore_wait(barrier, len(partners) + len(mirrors))


    def relay(entry):
        ch, dy, dz, children = entry
        origin = lax.rem(y - sign_y * dy + NY, NY) * NZ + lax.rem(z - sign_z * dz + NZ, NZ)
        piece = c_bufs[ch].at[pl.ds(origin * 4 + 2 * c, 2)]
        if dy or dz:
            copy(piece, piece, c_send.at[ch], c_recv.at[SLOT[ch, dy, dz]], sibling).wait_recv()
        for child_dy, child_dz, dx in children:
            to = at(dx=dx) if dx else at(dy=sign_y * (child_dy - dy), dz=sign_z * (child_dz - dz))
            copy(piece, piece, c_send.at[ch], c_recv.at[SLOT[ch, child_dy, child_dz]], to).start()
        if dy or dz:
            copy(piece, piece, cf_send.at[ch], cf_recv.at[ch], sibling).start()

    carried = c_buf0.at[pl.ds(0, 62)]

    def wait_flipped(ch):
        copy(carried, carried, cf_send.at[ch], cf_recv.at[ch], sibling).wait_recv()

    def build_rhs(ch):
        for k in range(32):
            block = c_bufs[ch][owner_ref[k] * 4 + tile_ref[k]]
            zero = jnp.zeros_like(block)
            for b in range(2):
                rhs[k * BLK:(k + 1) * BLK, b * BLK:(b + 1) * BLK] = jnp.where(mblock_ref[k] == b, block, zero)

    def half_dot(g):
        lhs = jnp.concatenate([t_buf[:, 4 * g + j].reshape(8 * BLK, BLK) for j in range(4)], axis=1)
        product = jnp.dot(lhs, rhs[g * 512:(g + 1) * 512, :], preferred_element_type=F32)
        if g == 0:
            acc[...] = product
        else:
            acc[...] += product

    def store_half(ch):
        for p in range(8):
            for b in range(2):
                h_own[ch, c, p // 2, b * BLK:(b + 1) * BLK, p % 2 * BLK:(p % 2 + 1) * BLK] = acc[
                    p * BLK:(p + 1) * BLK, b * BLK:(b + 1) * BLK
                ].astype(BF16)

    def send_nbr(ch, side):
        return copy(
            h_own.at[ch, c, pl.ds(2 * side, 2)], h_nbr.at[ch, side, c], n_send.at[ch, side], n_recv.at[ch, side],
            at(dx=1 if side else 3),
        )

    def send_far(ch, side):
        to = lax.rem(x + (1 if side else 3), NX)
        return copy(
            h_nbr.at[ch, side, c, to // 2], h_far.at[ch, side, c], f_send.at[ch, side], f_recv.at[ch, side],
            at(dx=1 if side else 3),
        )

    def flip_own(ch):
        ref = h_own.at[ch, c]
        return copy(ref, ref, of_send.at[ch], of_recv.at[ch], sibling)

    def flip_nbr(ch, side):
        ref = h_nbr.at[ch, side, c]
        return copy(ref, ref, nf_send.at[ch, side], nf_recv.at[ch, side], sibling)

    def flip_far(ch, side):
        ref = h_far.at[ch, side, c]
        return copy(ref, ref, ff_send.at[ch, side], ff_recv.at[ch, side], sibling)

    def gram(d):
        for src in range(2):
            total = None
            for ch in range(2):
                if d == 0:
                    terms = [(h_own[ch, src, q], h_own[ch, c, q]) for q in range(4)]
                elif d == 2:
                    terms = [(h_far[ch, j, src], h_own[ch, c, 2 * j + x // 2]) for j in range(2)]
                else:
                    side = d // 2
                    terms = [(h_nbr[ch, side, src, j], h_own[ch, c, 2 * side + j]) for j in range(2)]
                for rows, columns in terms:
                    part = lax.dot_general(rows, columns, (((1,), (1,)), ((), ())), preferred_element_type=F32)
                    total = part if total is None else total + part
            g_buf[src * 256:(src + 1) * 256, :] = total
            z_out[d, src * 256:(src + 1) * 256, :] = total.astype(BF16)
        y_sum[d] = g_buf[pl.ds(pl.multiple_of(z * 64, 64), 64), :]

    def z_copy(d, e):
        rows = pl.ds(pl.multiple_of(lax.rem(z + e, NZ) * 64, 64), 64)
        return copy(z_out.at[d, rows], z_in.at[d, e - 1], z_send.at[d], z_recv.at[d], at(dz=e))

    def z_start(d):
        for e in (4, 3, 5, 2, 6, 1, 7):
            z_copy(d, e).start()

    def y_copy(d):
        plane = lax.rem(x + d, NX)
        slot = lax.rem(y - plane + 2 * NY - 1, NY)
        to = {"aux": plane * NZ + z, "row": r}
        return plane, copy(y_sum.at[d], y_in.at[slot], y_send.at[d], y_recv.at[slot], to)

    def z_finish(d):
        copy(z_in.at[d], z_in.at[d], z_send.at[d], z_recv.at[d], sibling).wait_recv()
        total = y_sum[d]
        for e in range(NZ - 1):
            total = total + z_in[d, e].astype(F32)
        y_sum[d] = total
        plane, send = y_copy(d)
        pl.when(plane != y)(send.start)

    done = max(i for i, entry in enumerate(TREE) if entry[0] == 0) + 1
    for entry in TREE[:done]:
        relay(entry)
    later = list(TREE[done:])
    wait_flipped(0)
    t_copy.wait()
    build_rhs(0)
    for g in range(8):
        half_dot(g)
        if later:
            relay(later.pop(0))
    store_half(0)
    for side in range(2):
        send_nbr(0, side).start()
    flip_own(0).start()
    for entry in later:
        relay(entry)
    wait_flipped(1)
    build_rhs(1)
    for g in range(8):
        half_dot(g)
    store_half(1)
    for side in range(2):
        send_nbr(1, side).start()
    flip_own(1).start()
    for ch in range(2):
        for side in range(2):
            send_nbr(ch, side).wait_recv()
            send_far(ch, side).start()
            flip_nbr(ch, side).start()
        if ch == 0:
            for own in range(2):
                flip_own(own).wait_recv()
            gram(0)
            z_start(0)
    for side in range(2):
        for ch in range(2):
            flip_nbr(ch, side).wait_recv()
        gram(2 * side + 1)
        z_start(2 * side + 1)
    z_finish(0)
    for ch in range(2):
        for side in range(2):
            send_far(ch, side).wait_recv()
            flip_far(ch, side).start()
    for ch in range(2):
        for side in range(2):
            flip_far(ch, side).wait_recv()
    gram(2)
    z_start(2)
    for d in (1, 3, 2):
        z_finish(d)
    for slot in range(NY - 1):
        copy(y_in.at[slot], y_in.at[slot], y_send.at[0], y_recv.at[slot], sibling).wait_recv()
    total = y_sum[lax.rem(y - x + NY, NY)] + y_in[0] + y_in[1] + y_in[2]

    def mirror_copy(t):
        return copy(x_out.at[pl.ds(t * 64, 64)], x_in.at[lax.rem(z, 4)], x_send, x_recv, mirrors[t])

    out_ref[...] = total

    @pl.when(x != y)
    def _():
        x_pad[...] = jnp.zeros_like(x_pad)
        x_pad[pl.ds(pl.multiple_of(lax.rem(z, 2) * 64, 64), 64), :] = out_ref[...]
        x_out[...] = x_pad[...].T
        for t in range(4):
            mirror_copy(t).start()
        copy(x_in, x_in, x_send, x_recv, sibling).wait_recv()
        out_ref[:, 0:BLK] += x_in[0] + x_in[1]
        out_ref[:, BLK:2 * BLK] += x_in[2] + x_in[3]
        copy(x_in, x_in, x_send, x_recv, sibling).wait_send()

    for ch in range(2):
        copy(carried, carried, c_send.at[ch], c_recv.at[0], sibling).wait_send()
        copy(carried, carried, cf_send.at[ch], cf_recv.at[ch], sibling).wait_send()
        flip_own(ch).wait_send()
        for side in range(2):
            send_nbr(ch, side).wait_send()
            send_far(ch, side).wait_send()
            flip_nbr(ch, side).wait_send()
            flip_far(ch, side).wait_send()
    for d in range(NX):
        copy(z_in.at[d], z_in.at[d], z_send.at[d], z_recv.at[d], sibling).wait_send()
        plane, send = y_copy(d)
        pl.when(plane != y)(send.wait_send)


def shards(three_index, coeffs, pair_owner, pair_tile, pair_mblock):
    smem, vmem = pl.BlockSpec(memory_space=pltpu.SMEM), pl.BlockSpec(memory_space=pltpu.VMEM)
    dma = pltpu.SemaphoreType.DMA
    return pl.pallas_call(
        kernel,
        out_shape=jax.ShapeDtypeStruct((64, 256), F32),
        in_specs=[smem, smem, smem, vmem, pl.BlockSpec(memory_space=pl.ANY)],
        out_specs=vmem,
        scratch_shapes=[
            pltpu.VMEM((8, 32, BLK, BLK), BF16),
            pltpu.VMEM((128, BLK, BLK), BF16),
            pltpu.VMEM((128, BLK, BLK), BF16),
            pltpu.VMEM((32 * BLK, 256), BF16),
            pltpu.VMEM((8 * BLK, 256), F32),
            pltpu.VMEM((2, 2, 4, 256, 256), BF16),
            pltpu.VMEM((2, 2, 2, 2, 256, 256), BF16),
            pltpu.VMEM((2, 2, 2, 256, 256), BF16),
            pltpu.VMEM((512, 256), F32),
            pltpu.VMEM((4, 512, 256), BF16),
            pltpu.VMEM((4, 7, 64, 256), BF16),
            pltpu.VMEM((4, 64, 256), F32),
            pltpu.VMEM((4, 64, 256), F32),
            pltpu.VMEM((BLK, 256), F32),
            pltpu.VMEM((256, BLK), F32),
            pltpu.VMEM((4, 64, BLK), F32),
            dma, dma((64,)), dma((2,)), dma((2,)), dma((2,)),
            dma((2, 2)), dma((2, 2)), dma((2, 2)), dma((2, 2)), dma((2,)), dma((2,)),
            dma((2, 2)), dma((2, 2)), dma((2, 2)), dma((2, 2)),
            dma((4,)), dma((4,)), dma((4,)), dma((4,)), dma, dma,
        ],
        compiler_params=pltpu.CompilerParams(
            collective_id=0, has_side_effects=True, vmem_limit_bytes=56 * 1024 * 1024
        ),
        name="exchange",
    )(pair_owner.reshape(32), pair_tile.reshape(32), pair_mblock.reshape(32), coeffs, three_index)


def solution(mesh):
    placed = (
        P("aux", "row", None, None),
        P("aux", None),
        P("aux", "row", None),
        P("aux", "row"),
        P("aux", "row"),
    )
    return jax.shard_map(
        shards, mesh=mesh, in_specs=placed, out_specs=P("aux", "row"), check_vma=False
    )
```

```python
import jax
import jax.numpy as jnp
from jax import lax
from jax.experimental import pallas as pl
from jax.experimental.pallas import tpu as pltpu
from jax.sharding import PartitionSpec as P

MESH = pl.DeviceIdType.MESH
NX, NY, NZ = 4, 4, 8
BLK = 128
F32, BF16 = jnp.float32, jnp.bfloat16


TREE = (
    (0, 0, 0, ((0, 2, 0), (0, 6, 0), (1, 0, 0), (0, 7, 0),)),
    (1, 0, 0, ((3, 0, 0),)),
    (0, 1, 0, ((1, 1, 0), (2, 0, 0), (3, 0, 1),)),
    (1, 3, 0, ((3, 7, 0), (3, 3, 0), (1, 0, 1), (2, 0, 0),)),
    (0, 0, 2, ((3, 2, 0),)),
    (0, 0, 6, ((0, 4, 0), (0, 5, 0), (1, 6, 0), (3, 6, 0),)),
    (0, 0, 7, ((1, 7, 0),)),
    (0, 1, 1, ((3, 1, -1), (0, 1, 0),)),
    (0, 2, 0, ((2, 7, 0),)),
    (0, 3, 0, ()),
    (1, 3, 7, ((0, 7, 0), (1, 7, -1), (3, 5, 0), (2, 7, 0),)),
    (1, 2, 0, ()),
    (1, 1, 0, ((1, 1, 0),)),
    (0, 3, 2, ((3, 3, 0), (1, 2, 1), (2, 2, 0),)),
    (0, 1, 6, ((2, 6, 0),)),
    (0, 3, 6, ((3, 5, 0),)),
    (0, 1, 7, ((3, 7, 1),)),
    (0, 3, 1, ((2, 1, 0),)),
    (0, 0, 4, ((1, 4, 0), (0, 3, 0),)),
    (0, 0, 1, ()),
    (0, 0, 5, ((1, 5, 0), (2, 5, 0),)),
    (1, 0, 7, ((0, 1, 0),)),
    (1, 1, 7, ((1, 6, 0),)),
    (1, 3, 3, ((1, 3, -1),)),
    (1, 1, 1, ()),
    (0, 1, 2, ()),
    (1, 2, 7, ((2, 1, 0),)),
    (0, 2, 7, ()),
    (0, 2, 6, ()),
    (0, 3, 3, ((1, 3, -1), (2, 3, 0),)),
    (0, 3, 7, ()),
    (0, 2, 2, ()),
    (0, 1, 4, ((2, 4, 0), (3, 4, 1),)),
    (0, 2, 1, ()),
    (1, 1, 3, ((1, 2, 0), (1, 4, 0), (0, 3, 0), (2, 3, 0),)),
    (0, 1, 5, ()),
    (1, 3, 5, ((0, 5, 0), (2, 5, 0), (3, 4, 0),)),
    (0, 3, 5, ()),
    (1, 0, 1, ((0, 2, 0), (3, 1, 0),)),
    (0, 1, 3, ()),
    (0, 2, 5, ()),
    (0, 3, 4, ()),
    (0, 2, 3, ()),
    (0, 0, 3, ()),
    (0, 2, 4, ()),
    (1, 0, 3, ()),
    (1, 1, 6, ((2, 6, 0), (3, 6, -1),)),
    (1, 2, 3, ()),
    (1, 2, 1, ()),
    (1, 1, 4, ((0, 4, 0), (1, 5, 0),)),
    (1, 2, 5, ((2, 4, 0),)),
    (1, 1, 2, ((2, 2, 0),)),
    (1, 0, 5, ((0, 6, 0),)),
    (1, 0, 2, ((3, 2, 0),)),
    (1, 3, 1, ()),
    (1, 3, 4, ()),
    (1, 2, 6, ()),
    (1, 3, 6, ()),
    (1, 0, 4, ()),
    (1, 1, 5, ()),
    (1, 2, 4, ()),
    (1, 2, 2, ()),
    (1, 3, 2, ()),
    (1, 0, 6, ()),
)

SLOT = {entry[:3]: i for i, entry in enumerate(TREE)}


def kernel(
    owner_ref, tile_ref, mblock_ref, coef_ref, t_hbm, out_ref,
    t_buf, c_buf0, c_buf1, rhs, acc, h_own, h_nbr, h_far, g_buf, g_nbr, z_out, z_in, y_sum, y_in,
    w_in, w_out, v_in, x_pad, x_out, x_in,
    t_sem, c_recv, c_send, cf_recv, cf_send, n_recv, n_send, f_recv, f_send, of_recv, of_send, nf_recv, nf_send,
    ff_recv, ff_send, z_recv, z_send, y_recv, y_send,
    w_recv, w_send, v_recv, v_send, x_recv, x_send,
):
    a, r = lax.axis_index("aux"), lax.axis_index("row")
    y, z = a // NZ, lax.rem(a, NZ)
    x, c = r // 2, lax.rem(r, 2)
    sign_z = 1 - 2 * c
    sign_y = sign_z * (1 - 2 * lax.rem(x, 2))

    def at(dx=0, dy=0, dz=0, flip=0):
        return {
            "aux": lax.rem(y + dy + NY, NY) * NZ + lax.rem(z + dz + NZ, NZ),
            "row": lax.rem(x + dx + NX, NX) * 2 + lax.rem(c + flip, 2),
        }

    def copy(src, dst, send, recv, device):
        return pltpu.make_async_remote_copy(
            src_ref=src, dst_ref=dst, send_sem=send, recv_sem=recv, device_id=device, device_id_type=MESH
        )

    c_bufs = (c_buf0, c_buf1)
    sibling = at(flip=1)
    t_copy = pltpu.make_async_copy(t_hbm, t_buf, t_sem)
    t_copy.start()
    partners = [sibling]
    partners += [at(dx=e) for e in (1, 3)]
    partners += [at(dy=e) for e in range(1, NY)]
    partners += [at(dz=e) for e in range(1, NZ)]
    mirrors = [{"aux": x * NZ + 4 * c + t, "row": y * 2 + z // 4} for t in range(4)]
    barrier = pltpu.get_barrier_semaphore()
    for device in partners:
        pl.semaphore_signal(barrier, inc=1, device_id=device, device_id_type=MESH)

    @pl.when(x != y)
    def _():
        for device in mirrors:
            pl.semaphore_signal(barrier, inc=1, device_id=device, device_id_type=MESH)

    for ch in range(2):
        for t in range(4):
            c_bufs[ch][a * 4 + t] = coef_ref[t * BLK:(t + 1) * BLK, ch * BLK:(ch + 1) * BLK]

    @pl.when(x == y)
    def _():
        pl.semaphore_wait(barrier, len(partners))

    @pl.when(x != y)
    def _():
        pl.semaphore_wait(barrier, len(partners) + len(mirrors))


    def relay(entry):
        ch, dy, dz, children = entry
        origin = lax.rem(y - sign_y * dy + NY, NY) * NZ + lax.rem(z - sign_z * dz + NZ, NZ)
        piece = c_bufs[ch].at[pl.ds(origin * 4 + 2 * c, 2)]
        if dy or dz:
            copy(piece, piece, c_send.at[ch], c_recv.at[SLOT[ch, dy, dz]], sibling).wait_recv()
        for child_dy, child_dz, dx in children:
            to = at(dx=dx) if dx else at(dy=sign_y * (child_dy - dy), dz=sign_z * (child_dz - dz))
            copy(piece, piece, c_send.at[ch], c_recv.at[SLOT[ch, child_dy, child_dz]], to).start()
        if dy or dz:
            copy(piece, piece, cf_send.at[ch], cf_recv.at[ch], sibling).start()

    carried = c_buf0.at[pl.ds(0, 62)]

    def wait_flipped(ch):
        copy(carried, carried, cf_send.at[ch], cf_recv.at[ch], sibling).wait_recv()

    def build_rhs(ch):
        for k in range(32):
            block = c_bufs[ch][owner_ref[k] * 4 + tile_ref[k]]
            zero = jnp.zeros_like(block)
            for b in range(2):
                rhs[k * BLK:(k + 1) * BLK, b * BLK:(b + 1) * BLK] = jnp.where(mblock_ref[k] == b, block, zero)

    def half_dot(g):
        lhs = jnp.concatenate([t_buf[:, 4 * g + j].reshape(8 * BLK, BLK) for j in range(4)], axis=1)
        product = jnp.dot(lhs, rhs[g * 512:(g + 1) * 512, :], preferred_element_type=F32)
        if g == 0:
            acc[...] = product
        else:
            acc[...] += product

    def store_half(ch):
        for p in range(8):
            for b in range(2):
                h_own[ch, c, p // 2, b * BLK:(b + 1) * BLK, p % 2 * BLK:(p % 2 + 1) * BLK] = acc[
                    p * BLK:(p + 1) * BLK, b * BLK:(b + 1) * BLK
                ].astype(BF16)

    def send_nbr(ch, side):
        return copy(
            h_own.at[ch, c, pl.ds(2 * side, 2)], h_nbr.at[ch, side, c], n_send.at[ch, side], n_recv.at[ch, side],
            at(dx=1 if side else 3),
        )

    def send_far(ch, side):
        to = lax.rem(x + (1 if side else 3), NX)
        return copy(
            h_nbr.at[ch, side, c, to // 2], h_far.at[ch, side, c], f_send.at[ch, side], f_recv.at[ch, side],
            at(dx=1 if side else 3),
        )

    def flip_own(ch):
        ref = h_own.at[ch, c]
        return copy(ref, ref, of_send.at[ch], of_recv.at[ch], sibling)

    def flip_nbr(ch, side):
        ref = h_nbr.at[ch, side, c]
        return copy(ref, ref, nf_send.at[ch, side], nf_recv.at[ch, side], sibling)

    def flip_far(ch, side):
        ref = h_far.at[ch, side, c]
        return copy(ref, ref, ff_send.at[ch, side], ff_recv.at[ch, side], sibling)

    def gram(d, src):
        total = None
        for ch in range(2):
            if d == 0:
                terms = [(h_own[ch, src, q], h_own[ch, c, q]) for q in range(4)]
            elif d == 2:
                terms = [(h_far[ch, j, src], h_own[ch, c, 2 * j + x // 2]) for j in range(2)]
            else:
                side = d // 2
                terms = [(h_nbr[ch, side, src, j], h_own[ch, c, 2 * side + j]) for j in range(2)]
            for rows, columns in terms:
                part = lax.dot_general(rows, columns, (((1,), (1,)), ((), ())), preferred_element_type=F32)
                total = part if total is None else total + part
        rows = pl.ds(pl.multiple_of(src * 256, 256), 256)
        if d % 2:
            g_nbr[d // 2, rows, :] = total
        else:
            g_buf[rows, :] = total
        z_out[d, rows, :] = total.astype(BF16)

    cores = (c, lax.rem(c + 1, 2))
    own_rows = pl.ds(pl.multiple_of(z * 64, 64), 64)

    def z_start(d, src):
        for t in range(4):
            to = 4 * src + t
            rows = pl.ds(pl.multiple_of(to * 64, 64), 64)
            send = copy(
                z_out.at[d, rows], z_in.at[d, lax.rem(to - z + 2 * NZ - 1, NZ)], z_send.at[d], z_recv.at[d],
                {"aux": y * NZ + to, "row": r},
            )
            pl.when(to != z)(send.start)

    def w_copy(d, rows):
        plane = lax.rem(x + d, NX)
        slot = lax.rem(y - plane + 2 * NY - 1, NY)
        to = {"aux": plane * NZ + z, "row": r}
        return plane, copy(z_out.at[d, rows], w_in.at[slot, rows], w_send.at[d // 2], w_recv.at[slot], to)

    def w_start(d, src):
        plane, send = w_copy(d, pl.ds(pl.multiple_of(src * 256, 256), 256))
        pl.when(plane != y)(send.start)

    def v_copy(e):
        rows = pl.ds(pl.multiple_of(lax.rem(z + e, NZ) * 64, 64), 64)
        return copy(w_out.at[rows], v_in.at[e - 1], v_send, v_recv, at(dz=e))

    near = lax.rem(x + y, 2) == 1

    def w_finish():
        for slot in range(NY - 1):
            copy(w_in.at[slot], w_in.at[slot], w_send.at[0], w_recv.at[slot], sibling).wait_recv()
        total = g_nbr[lax.rem(y - x + NY, NY) // 2]
        for slot in range(NY - 1):
            total = total + w_in[slot].astype(F32)
        w_out[...] = total.astype(BF16)
        g_nbr[0] = total
        for e in (4, 3, 5, 2, 6, 1, 7):
            v_copy(e).start()
        y_sum[1] = g_nbr[0, own_rows, :]

    def v_finish():
        copy(v_in, v_in, v_send, v_recv, sibling).wait_recv()
        total = y_sum[1]
        for e in range(NZ - 1):
            total = total + v_in[e].astype(F32)
        out_ref[...] = total

    def y_finish():
        for slot in range(NY - 1):
            copy(y_in.at[slot], y_in.at[slot], y_send.at[0], y_recv.at[slot], sibling).wait_recv()
        out_ref[...] = y_sum[lax.rem(y - x + NY, NY)] + y_in[0] + y_in[1] + y_in[2]

    def y_copy(d):
        plane = lax.rem(x + d, NX)
        slot = lax.rem(y - plane + 2 * NY - 1, NY)
        to = {"aux": plane * NZ + z, "row": r}
        return plane, copy(y_sum.at[d], y_in.at[slot], y_send.at[d], y_recv.at[slot], to)

    def z_finish(d):
        copy(z_in.at[d], z_in.at[d], z_send.at[d], z_recv.at[d], sibling).wait_recv()
        total = y_sum[d]
        for e in range(NZ - 1):
            total = total + z_in[d, e].astype(F32)
        y_sum[d] = total
        plane, send = y_copy(d)
        pl.when(plane != y)(send.start)

    done = max(i for i, entry in enumerate(TREE) if entry[0] == 0) + 1
    for entry in TREE[:done]:
        relay(entry)
    later = list(TREE[done:])
    wait_flipped(0)
    t_copy.wait()
    build_rhs(0)
    for g in range(8):
        half_dot(g)
        if later:
            relay(later.pop(0))
    store_half(0)
    for side in range(2):
        send_nbr(0, side).start()
    flip_own(0).start()
    for entry in later:
        relay(entry)
    wait_flipped(1)
    build_rhs(1)
    for g in range(8):
        half_dot(g)
    store_half(1)
    for side in range(2):
        send_nbr(1, side).start()
    flip_own(1).start()
    for ch in range(2):
        for side in range(2):
            send_nbr(ch, side).wait_recv()
            flip_nbr(ch, side).start()
            send_far(ch, side).start()
        if ch == 0:
            for own in range(2):
                flip_own(own).wait_recv()
            for src in range(2):
                gram(0, src)
                z_start(0, src)
            y_sum[0] = g_buf[own_rows, :]
    for side in range(2):
        gram(2 * side + 1, cores[0])
        w_start(2 * side + 1, cores[0])
    for side in range(2):
        for ch in range(2):
            flip_nbr(ch, side).wait_recv()
        gram(2 * side + 1, cores[1])
        w_start(2 * side + 1, cores[1])
    z_finish(0)
    for ch in range(2):
        for side in range(2):
            send_far(ch, side).wait_recv()
            flip_far(ch, side).start()
    gram(2, cores[0])
    z_start(2, cores[0])
    for ch in range(2):
        for side in range(2):
            flip_far(ch, side).wait_recv()
    gram(2, cores[1])
    z_start(2, cores[1])
    y_sum[2] = g_buf[own_rows, :]
    pl.when(near)(w_finish)
    z_finish(2)
    pl.when(near)(v_finish)
    pl.when(jnp.logical_not(near))(y_finish)

    def mirror_copy(t):
        return copy(x_out.at[pl.ds(t * 64, 64)], x_in.at[lax.rem(z, 4)], x_send, x_recv, mirrors[t])

    @pl.when(x != y)
    def _():
        x_pad[...] = jnp.zeros_like(x_pad)
        x_pad[pl.ds(pl.multiple_of(lax.rem(z, 2) * 64, 64), 64), :] = out_ref[...]
        x_out[...] = x_pad[...].T
        for t in range(4):
            mirror_copy(t).start()
        copy(x_in, x_in, x_send, x_recv, sibling).wait_recv()
        out_ref[:, 0:BLK] += x_in[0] + x_in[1]
        out_ref[:, BLK:2 * BLK] += x_in[2] + x_in[3]
        copy(x_in, x_in, x_send, x_recv, sibling).wait_send()

    for ch in range(2):
        copy(carried, carried, c_send.at[ch], c_recv.at[0], sibling).wait_send()
        copy(carried, carried, cf_send.at[ch], cf_recv.at[ch], sibling).wait_send()
        flip_own(ch).wait_send()
        for side in range(2):
            send_nbr(ch, side).wait_send()
            send_far(ch, side).wait_send()
            flip_nbr(ch, side).wait_send()
            flip_far(ch, side).wait_send()
    for d in (0, 2):
        copy(z_in.at[d], z_in.at[d], z_send.at[d], z_recv.at[d], sibling).wait_send()
        plane, send = y_copy(d)
        pl.when(plane != y)(send.wait_send)
    for d in (1, 3):
        plane, send = w_copy(d, pl.ds(0, 512))
        pl.when(plane != y)(send.wait_send)
    pl.when(near)(copy(v_in, v_in, v_send, v_recv, sibling).wait_send)


def shards(three_index, coeffs, pair_owner, pair_tile, pair_mblock):
    smem, vmem = pl.BlockSpec(memory_space=pltpu.SMEM), pl.BlockSpec(memory_space=pltpu.VMEM)
    dma = pltpu.SemaphoreType.DMA
    return pl.pallas_call(
        kernel,
        out_shape=jax.ShapeDtypeStruct((64, 256), F32),
        in_specs=[smem, smem, smem, vmem, pl.BlockSpec(memory_space=pl.ANY)],
        out_specs=vmem,
        scratch_shapes=[
            pltpu.VMEM((8, 32, BLK, BLK), BF16),
            pltpu.VMEM((128, BLK, BLK), BF16),
            pltpu.VMEM((128, BLK, BLK), BF16),
            pltpu.VMEM((32 * BLK, 256), BF16),
            pltpu.VMEM((8 * BLK, 256), F32),
            pltpu.VMEM((2, 2, 4, 256, 256), BF16),
            pltpu.VMEM((2, 2, 2, 2, 256, 256), BF16),
            pltpu.VMEM((2, 2, 2, 256, 256), BF16),
            pltpu.VMEM((512, 256), F32),
            pltpu.VMEM((2, 512, 256), F32),
            pltpu.VMEM((4, 512, 256), BF16),
            pltpu.VMEM((4, 7, 64, 256), BF16),
            pltpu.VMEM((4, 64, 256), F32),
            pltpu.VMEM((4, 64, 256), F32),
            pltpu.VMEM((4, 512, 256), BF16),
            pltpu.VMEM((512, 256), BF16),
            pltpu.VMEM((7, 64, 256), BF16),
            pltpu.VMEM((BLK, 256), F32),
            pltpu.VMEM((256, BLK), F32),
            pltpu.VMEM((4, 64, BLK), F32),
            dma, dma((64,)), dma((2,)), dma((2,)), dma((2,)),
            dma((2, 2)), dma((2, 2)), dma((2, 2)), dma((2, 2)), dma((2,)), dma((2,)),
            dma((2, 2)), dma((2, 2)), dma((2, 2)), dma((2, 2)),
            dma((4,)), dma((4,)), dma((4,)), dma((4,)),
            dma((4,)), dma((2,)), dma, dma, dma, dma,
        ],
        compiler_params=pltpu.CompilerParams(
            collective_id=0, has_side_effects=True, vmem_limit_bytes=56 * 1024 * 1024
        ),
        name="exchange",
    )(pair_owner.reshape(32), pair_tile.reshape(32), pair_mblock.reshape(32), coeffs, three_index)


def solution(mesh):
    placed = (
        P("aux", "row", None, None),
        P("aux", None),
        P("aux", "row", None),
        P("aux", "row"),
        P("aux", "row"),
    )
    return jax.shard_map(
        shards, mesh=mesh, in_specs=placed, out_specs=P("aux", "row"), check_vma=False
    )
```

```python
import jax
import jax.numpy as jnp
from jax import lax
from jax.experimental import pallas as pl
from jax.experimental.pallas import tpu as pltpu
from jax.sharding import PartitionSpec as P

MESH = pl.DeviceIdType.MESH
NX, NY, NZ = 4, 4, 8
BLK = 128
F32, BF16 = jnp.float32, jnp.bfloat16


TREE = (
    (0, 0, 0, ((0, 2, 0), (0, 6, 0), (1, 0, 0), (0, 7, 0),)),
    (1, 0, 0, ((3, 0, 0),)),
    (0, 1, 0, ((1, 1, 0), (2, 0, 0), (3, 0, 1),)),
    (1, 3, 0, ((3, 7, 0), (3, 3, 0), (1, 0, 1), (2, 0, 0),)),
    (0, 0, 2, ((3, 2, 0),)),
    (0, 0, 6, ((0, 4, 0), (0, 5, 0), (1, 6, 0), (3, 6, 0),)),
    (0, 0, 7, ((1, 7, 0),)),
    (0, 1, 1, ((3, 1, -1), (0, 1, 0),)),
    (0, 2, 0, ((2, 7, 0),)),
    (0, 3, 0, ()),
    (1, 3, 7, ((0, 7, 0), (1, 7, -1), (3, 5, 0), (2, 7, 0),)),
    (1, 2, 0, ()),
    (1, 1, 0, ((1, 1, 0),)),
    (0, 3, 2, ((3, 3, 0), (1, 2, 1), (2, 2, 0),)),
    (0, 1, 6, ((2, 6, 0),)),
    (0, 3, 6, ((3, 5, 0),)),
    (0, 1, 7, ((3, 7, 1),)),
    (0, 3, 1, ((2, 1, 0),)),
    (0, 0, 4, ((1, 4, 0), (0, 3, 0),)),
    (0, 0, 1, ()),
    (0, 0, 5, ((1, 5, 0), (2, 5, 0),)),
    (1, 0, 7, ((0, 1, 0),)),
    (1, 1, 7, ((1, 6, 0),)),
    (1, 3, 3, ((1, 3, -1),)),
    (1, 1, 1, ()),
    (0, 1, 2, ()),
    (1, 2, 7, ((2, 1, 0),)),
    (0, 2, 7, ()),
    (0, 2, 6, ()),
    (0, 3, 3, ((1, 3, -1), (2, 3, 0),)),
    (0, 3, 7, ()),
    (0, 2, 2, ()),
    (0, 1, 4, ((2, 4, 0), (3, 4, 1),)),
    (0, 2, 1, ()),
    (1, 1, 3, ((1, 2, 0), (1, 4, 0), (0, 3, 0), (2, 3, 0),)),
    (0, 1, 5, ()),
    (1, 3, 5, ((0, 5, 0), (2, 5, 0), (3, 4, 0),)),
    (0, 3, 5, ()),
    (1, 0, 1, ((0, 2, 0), (3, 1, 0),)),
    (0, 1, 3, ()),
    (0, 2, 5, ()),
    (0, 3, 4, ()),
    (0, 2, 3, ()),
    (0, 0, 3, ()),
    (0, 2, 4, ()),
    (1, 0, 3, ()),
    (1, 1, 6, ((2, 6, 0), (3, 6, -1),)),
    (1, 2, 3, ()),
    (1, 2, 1, ()),
    (1, 1, 4, ((0, 4, 0), (1, 5, 0),)),
    (1, 2, 5, ((2, 4, 0),)),
    (1, 1, 2, ((2, 2, 0),)),
    (1, 0, 5, ((0, 6, 0),)),
    (1, 0, 2, ((3, 2, 0),)),
    (1, 3, 1, ()),
    (1, 3, 4, ()),
    (1, 2, 6, ()),
    (1, 3, 6, ()),
    (1, 0, 4, ()),
    (1, 1, 5, ()),
    (1, 2, 4, ()),
    (1, 2, 2, ()),
    (1, 3, 2, ()),
    (1, 0, 6, ()),
)

SLOT = {entry[:3]: i for i, entry in enumerate(TREE)}


def kernel(
    owner_ref, tile_ref, mblock_ref, coef_ref, t_hbm, out_ref,
    t_buf, c_buf0, c_buf1, rhs, acc, h_own, h_nbr, h_far, g_buf, g_nbr, z_out, z_in, y_sum, y_in,
    w_in, w_out, v_in, x_pad, x_out, x_in,
    t_sem, c_recv, c_send, cf_recv, cf_send, n_recv, n_send, f_recv, f_send, of_recv, of_send, nf_recv, nf_send,
    ff_recv, ff_send, z_recv, z_send, y_recv, y_send,
    w_recv, w_send, v_recv, v_send, x_recv, x_send,
):
    a, r = lax.axis_index("aux"), lax.axis_index("row")
    y, z = a // NZ, lax.rem(a, NZ)
    x, c = r // 2, lax.rem(r, 2)
    sign_z = 1 - 2 * c
    sign_y = sign_z * (1 - 2 * lax.rem(x, 2))

    def at(dx=0, dy=0, dz=0, flip=0):
        return {
            "aux": lax.rem(y + dy + NY, NY) * NZ + lax.rem(z + dz + NZ, NZ),
            "row": lax.rem(x + dx + NX, NX) * 2 + lax.rem(c + flip, 2),
        }

    def copy(src, dst, send, recv, device):
        return pltpu.make_async_remote_copy(
            src_ref=src, dst_ref=dst, send_sem=send, recv_sem=recv, device_id=device, device_id_type=MESH
        )

    c_bufs = (c_buf0, c_buf1)
    sibling = at(flip=1)
    t_copy = pltpu.make_async_copy(t_hbm, t_buf, t_sem)
    t_copy.start()
    partners = [sibling]
    partners += [at(dx=e) for e in (1, 3)]
    partners += [at(dy=e) for e in range(1, NY)]
    partners += [at(dz=e) for e in range(1, NZ)]
    mirrors = [{"aux": x * NZ + 4 * c + t, "row": y * 2 + z // 4} for t in range(4)]
    barrier = pltpu.get_barrier_semaphore()
    for device in partners:
        pl.semaphore_signal(barrier, inc=1, device_id=device, device_id_type=MESH)

    @pl.when(x != y)
    def _():
        for device in mirrors:
            pl.semaphore_signal(barrier, inc=1, device_id=device, device_id_type=MESH)

    for ch in range(2):
        for t in range(4):
            c_bufs[ch][a * 4 + t] = coef_ref[t * BLK:(t + 1) * BLK, ch * BLK:(ch + 1) * BLK]

    @pl.when(x == y)
    def _():
        pl.semaphore_wait(barrier, len(partners))

    @pl.when(x != y)
    def _():
        pl.semaphore_wait(barrier, len(partners) + len(mirrors))


    def relay(entry):
        ch, dy, dz, children = entry
        origin = lax.rem(y - sign_y * dy + NY, NY) * NZ + lax.rem(z - sign_z * dz + NZ, NZ)
        piece = c_bufs[ch].at[pl.ds(origin * 4 + 2 * c, 2)]
        if dy or dz:
            copy(piece, piece, c_send.at[ch], c_recv.at[SLOT[ch, dy, dz]], sibling).wait_recv()
        for child_dy, child_dz, dx in children:
            to = at(dx=dx) if dx else at(dy=sign_y * (child_dy - dy), dz=sign_z * (child_dz - dz))
            copy(piece, piece, c_send.at[ch], c_recv.at[SLOT[ch, child_dy, child_dz]], to).start()
        if dy or dz:
            copy(piece, piece, cf_send.at[ch], cf_recv.at[ch], sibling).start()

    carried = c_buf0.at[pl.ds(0, 62)]

    def wait_flipped(ch):
        copy(carried, carried, cf_send.at[ch], cf_recv.at[ch], sibling).wait_recv()

    def build_rhs(ch):
        for k in range(32):
            block = c_bufs[ch][owner_ref[k] * 4 + tile_ref[k]]
            zero = jnp.zeros_like(block)
            for b in range(2):
                rhs[k * BLK:(k + 1) * BLK, b * BLK:(b + 1) * BLK] = jnp.where(mblock_ref[k] == b, block, zero)

    def half_dot(g):
        lhs = jnp.concatenate([t_buf[:, 4 * g + j].reshape(8 * BLK, BLK) for j in range(4)], axis=1)
        product = jnp.dot(lhs, rhs[g * 512:(g + 1) * 512, :], preferred_element_type=F32)
        if g == 0:
            acc[...] = product
        else:
            acc[...] += product

    def store_half(ch):
        for p in range(8):
            for b in range(2):
                h_own[ch, c, p // 2, b * BLK:(b + 1) * BLK, p % 2 * BLK:(p % 2 + 1) * BLK] = acc[
                    p * BLK:(p + 1) * BLK, b * BLK:(b + 1) * BLK
                ].astype(BF16)

    def send_nbr(ch, side):
        return copy(
            h_own.at[ch, c, pl.ds(2 * side, 2)], h_nbr.at[ch, side, c], n_send.at[ch, side], n_recv.at[ch, side],
            at(dx=1 if side else 3),
        )

    def send_far(ch, side):
        to = lax.rem(x + (1 if side else 3), NX)
        return copy(
            h_nbr.at[ch, side, c, to // 2], h_far.at[ch, side, c], f_send.at[ch, side], f_recv.at[ch, side],
            at(dx=1 if side else 3),
        )

    def flip_own(ch):
        ref = h_own.at[ch, c]
        return copy(ref, ref, of_send.at[ch], of_recv.at[ch], sibling)

    def flip_nbr(ch, side):
        ref = h_nbr.at[ch, side, c]
        return copy(ref, ref, nf_send.at[ch, side], nf_recv.at[ch, side], sibling)

    def flip_far(ch, side):
        ref = h_far.at[ch, side, c]
        return copy(ref, ref, ff_send.at[ch, side], ff_recv.at[ch, side], sibling)

    def gram(d, src):
        total = None
        for ch in range(2):
            if d == 0:
                terms = [(h_own[ch, src, q], h_own[ch, c, q]) for q in range(4)]
            elif d == 2:
                terms = [(h_far[ch, j, src], h_own[ch, c, 2 * j + x // 2]) for j in range(2)]
            else:
                side = d // 2
                terms = [(h_nbr[ch, side, src, j], h_own[ch, c, 2 * side + j]) for j in range(2)]
            for rows, columns in terms:
                part = lax.dot_general(rows, columns, (((1,), (1,)), ((), ())), preferred_element_type=F32)
                total = part if total is None else total + part
        rows = pl.ds(pl.multiple_of(src * 256, 256), 256)
        if d % 2:
            g_nbr[d // 2, rows, :] = total
        else:
            g_buf[rows, :] = total
        z_out[d, rows, :] = total.astype(BF16)

    cores = (c, lax.rem(c + 1, 2))
    own_rows = pl.ds(pl.multiple_of(z * 64, 64), 64)

    def z_start(d, src):
        for t in range(4):
            to = 4 * src + t
            rows = pl.ds(pl.multiple_of(to * 64, 64), 64)
            send = copy(
                z_out.at[d, rows], z_in.at[d, lax.rem(to - z + 2 * NZ - 1, NZ)], z_send.at[d], z_recv.at[d],
                {"aux": y * NZ + to, "row": r},
            )
            pl.when(to != z)(send.start)

    def w_copy(d, rows):
        plane = lax.rem(x + d, NX)
        slot = lax.rem(y - plane + 2 * NY - 1, NY)
        to = {"aux": plane * NZ + z, "row": r}
        return plane, copy(z_out.at[d, rows], w_in.at[slot, rows], w_send.at[d // 2], w_recv.at[slot], to)

    def w_start(d, src):
        plane, send = w_copy(d, pl.ds(pl.multiple_of(src * 256, 256), 256))
        pl.when(plane != y)(send.start)

    def v_copy(e):
        rows = pl.ds(pl.multiple_of(lax.rem(z + e, NZ) * 64, 64), 64)
        return copy(w_out.at[rows], v_in.at[e - 1], v_send, v_recv, at(dz=e))

    near = lax.rem(x + y, 2) == 1

    def w_finish():
        for slot in range(NY - 1):
            copy(w_in.at[slot], w_in.at[slot], w_send.at[0], w_recv.at[slot], sibling).wait_recv()
        total = g_nbr[lax.rem(y - x + NY, NY) // 2]
        for slot in range(NY - 1):
            total = total + w_in[slot].astype(F32)
        w_out[...] = total.astype(BF16)
        g_nbr[0] = total
        for e in (4, 3, 5, 2, 6, 1, 7):
            v_copy(e).start()
        y_sum[1] = g_nbr[0, own_rows, :]

    def v_finish():
        copy(v_in, v_in, v_send, v_recv, sibling).wait_recv()
        total = y_sum[1]
        for e in range(NZ - 1):
            total = total + v_in[e].astype(F32)
        out_ref[...] = total

    def y_finish():
        for slot in range(NY - 1):
            copy(y_in.at[slot], y_in.at[slot], y_send.at[0], y_recv.at[slot], sibling).wait_recv()
        out_ref[...] = y_sum[lax.rem(y - x + NY, NY)] + y_in[0] + y_in[1] + y_in[2]

    def y_copy(d):
        plane = lax.rem(x + d, NX)
        slot = lax.rem(y - plane + 2 * NY - 1, NY)
        to = {"aux": plane * NZ + z, "row": r}
        return plane, copy(y_sum.at[d], y_in.at[slot], y_send.at[d], y_recv.at[slot], to)

    def z_finish(d):
        copy(z_in.at[d], z_in.at[d], z_send.at[d], z_recv.at[d], sibling).wait_recv()
        total = y_sum[d]
        for e in range(NZ - 1):
            total = total + z_in[d, e].astype(F32)
        y_sum[d] = total
        plane, send = y_copy(d)
        pl.when(plane != y)(send.start)

    done = max(i for i, entry in enumerate(TREE) if entry[0] == 0) + 1
    for entry in TREE[:done]:
        relay(entry)
    later = list(TREE[done:])
    wait_flipped(0)
    t_copy.wait()
    build_rhs(0)
    for g in range(8):
        half_dot(g)
        for _ in range(2):
            if later:
                relay(later.pop(0))
    store_half(0)
    for side in range(2):
        send_nbr(0, side).start()
    flip_own(0).start()
    for entry in later:
        relay(entry)
    wait_flipped(1)
    build_rhs(1)
    for g in range(8):
        half_dot(g)
    store_half(1)
    for side in range(2):
        send_nbr(1, side).start()
    flip_own(1).start()
    for ch in range(2):
        for side in range(2):
            send_nbr(ch, side).wait_recv()
            flip_nbr(ch, side).start()
            send_far(ch, side).start()
        if ch == 0:
            for own in range(2):
                flip_own(own).wait_recv()
            for src in range(2):
                gram(0, src)
                z_start(0, src)
            y_sum[0] = g_buf[own_rows, :]
    for side in range(2):
        gram(2 * side + 1, cores[0])
        w_start(2 * side + 1, cores[0])
    for side in range(2):
        for ch in range(2):
            flip_nbr(ch, side).wait_recv()
        gram(2 * side + 1, cores[1])
        w_start(2 * side + 1, cores[1])
    z_finish(0)
    for ch in range(2):
        for side in range(2):
            send_far(ch, side).wait_recv()
            flip_far(ch, side).start()
    gram(2, cores[0])
    z_start(2, cores[0])
    for ch in range(2):
        for side in range(2):
            flip_far(ch, side).wait_recv()
    gram(2, cores[1])
    z_start(2, cores[1])
    y_sum[2] = g_buf[own_rows, :]
    pl.when(near)(w_finish)
    z_finish(2)
    pl.when(near)(v_finish)
    pl.when(jnp.logical_not(near))(y_finish)

    def mirror_copy(t):
        return copy(x_out.at[pl.ds(t * 64, 64)], x_in.at[lax.rem(z, 4)], x_send, x_recv, mirrors[t])

    @pl.when(x != y)
    def _():
        x_pad[...] = jnp.zeros_like(x_pad)
        x_pad[pl.ds(pl.multiple_of(lax.rem(z, 2) * 64, 64), 64), :] = out_ref[...]
        x_out[...] = x_pad[...].T
        for t in range(4):
            mirror_copy(t).start()
        copy(x_in, x_in, x_send, x_recv, sibling).wait_recv()
        out_ref[:, 0:BLK] += x_in[0] + x_in[1]
        out_ref[:, BLK:2 * BLK] += x_in[2] + x_in[3]
        copy(x_in, x_in, x_send, x_recv, sibling).wait_send()

    for ch in range(2):
        copy(carried, carried, c_send.at[ch], c_recv.at[0], sibling).wait_send()
        copy(carried, carried, cf_send.at[ch], cf_recv.at[ch], sibling).wait_send()
        flip_own(ch).wait_send()
        for side in range(2):
            send_nbr(ch, side).wait_send()
            send_far(ch, side).wait_send()
            flip_nbr(ch, side).wait_send()
            flip_far(ch, side).wait_send()
    for d in (0, 2):
        copy(z_in.at[d], z_in.at[d], z_send.at[d], z_recv.at[d], sibling).wait_send()
        plane, send = y_copy(d)
        pl.when(plane != y)(send.wait_send)
    for d in (1, 3):
        plane, send = w_copy(d, pl.ds(0, 512))
        pl.when(plane != y)(send.wait_send)
    pl.when(near)(copy(v_in, v_in, v_send, v_recv, sibling).wait_send)


def shards(three_index, coeffs, pair_owner, pair_tile, pair_mblock):
    smem, vmem = pl.BlockSpec(memory_space=pltpu.SMEM), pl.BlockSpec(memory_space=pltpu.VMEM)
    dma = pltpu.SemaphoreType.DMA
    return pl.pallas_call(
        kernel,
        out_shape=jax.ShapeDtypeStruct((64, 256), F32),
        in_specs=[smem, smem, smem, vmem, pl.BlockSpec(memory_space=pl.ANY)],
        out_specs=vmem,
        scratch_shapes=[
            pltpu.VMEM((8, 32, BLK, BLK), BF16),
            pltpu.VMEM((128, BLK, BLK), BF16),
            pltpu.VMEM((128, BLK, BLK), BF16),
            pltpu.VMEM((32 * BLK, 256), BF16),
            pltpu.VMEM((8 * BLK, 256), F32),
            pltpu.VMEM((2, 2, 4, 256, 256), BF16),
            pltpu.VMEM((2, 2, 2, 2, 256, 256), BF16),
            pltpu.VMEM((2, 2, 2, 256, 256), BF16),
            pltpu.VMEM((512, 256), F32),
            pltpu.VMEM((2, 512, 256), F32),
            pltpu.VMEM((4, 512, 256), BF16),
            pltpu.VMEM((4, 7, 64, 256), BF16),
            pltpu.VMEM((4, 64, 256), F32),
            pltpu.VMEM((4, 64, 256), F32),
            pltpu.VMEM((4, 512, 256), BF16),
            pltpu.VMEM((512, 256), BF16),
            pltpu.VMEM((7, 64, 256), BF16),
            pltpu.VMEM((BLK, 256), F32),
            pltpu.VMEM((256, BLK), F32),
            pltpu.VMEM((4, 64, BLK), F32),
            dma, dma((64,)), dma((2,)), dma((2,)), dma((2,)),
            dma((2, 2)), dma((2, 2)), dma((2, 2)), dma((2, 2)), dma((2,)), dma((2,)),
            dma((2, 2)), dma((2, 2)), dma((2, 2)), dma((2, 2)),
            dma((4,)), dma((4,)), dma((4,)), dma((4,)),
            dma((4,)), dma((2,)), dma, dma, dma, dma,
        ],
        compiler_params=pltpu.CompilerParams(
            collective_id=0, has_side_effects=True, vmem_limit_bytes=56 * 1024 * 1024
        ),
        name="exchange",
    )(pair_owner.reshape(32), pair_tile.reshape(32), pair_mblock.reshape(32), coeffs, three_index)


def solution(mesh):
    placed = (
        P("aux", "row", None, None),
        P("aux", None),
        P("aux", "row", None),
        P("aux", "row"),
        P("aux", "row"),
    )
    return jax.shard_map(
        shards, mesh=mesh, in_specs=placed, out_specs=P("aux", "row"), check_vma=False
    )
```

```python
import jax
import jax.numpy as jnp
from jax import lax
from jax.experimental import pallas as pl
from jax.experimental.pallas import tpu as pltpu
from jax.sharding import PartitionSpec as P

MESH = pl.DeviceIdType.MESH
NX, NY, NZ = 4, 4, 8
BLK = 128
F32, BF16 = jnp.float32, jnp.bfloat16


TREE = (
    (0, 0, 0, ((0, 2, 0), (0, 6, 0), (1, 0, 0), (0, 7, 0),)),
    (1, 0, 0, ((3, 0, 0),)),
    (0, 1, 0, ((1, 1, 0), (2, 0, 0), (3, 0, 1),)),
    (1, 3, 0, ((3, 7, 0), (3, 3, 0), (1, 0, 1), (2, 0, 0),)),
    (0, 0, 2, ((3, 2, 0),)),
    (0, 0, 6, ((0, 4, 0), (0, 5, 0), (1, 6, 0), (3, 6, 0),)),
    (0, 0, 7, ((1, 7, 0),)),
    (0, 1, 1, ((3, 1, -1), (0, 1, 0),)),
    (0, 2, 0, ((2, 7, 0),)),
    (0, 3, 0, ()),
    (1, 3, 7, ((0, 7, 0), (1, 7, -1), (3, 5, 0), (2, 7, 0),)),
    (1, 2, 0, ()),
    (1, 1, 0, ((1, 1, 0),)),
    (0, 3, 2, ((3, 3, 0), (1, 2, 1), (2, 2, 0),)),
    (0, 1, 6, ((2, 6, 0),)),
    (0, 3, 6, ((3, 5, 0),)),
    (0, 1, 7, ((3, 7, 1),)),
    (0, 3, 1, ((2, 1, 0),)),
    (0, 0, 4, ((1, 4, 0), (0, 3, 0),)),
    (0, 0, 1, ()),
    (0, 0, 5, ((1, 5, 0), (2, 5, 0),)),
    (1, 0, 7, ((0, 1, 0),)),
    (1, 1, 7, ((1, 6, 0),)),
    (1, 3, 3, ((1, 3, -1),)),
    (1, 1, 1, ()),
    (0, 1, 2, ()),
    (1, 2, 7, ((2, 1, 0),)),
    (0, 2, 7, ()),
    (0, 2, 6, ()),
    (0, 3, 3, ((1, 3, -1), (2, 3, 0),)),
    (0, 3, 7, ()),
    (0, 2, 2, ()),
    (0, 1, 4, ((2, 4, 0), (3, 4, 1),)),
    (0, 2, 1, ()),
    (1, 1, 3, ((1, 2, 0), (1, 4, 0), (0, 3, 0), (2, 3, 0),)),
    (0, 1, 5, ()),
    (1, 3, 5, ((0, 5, 0), (2, 5, 0), (3, 4, 0),)),
    (0, 3, 5, ()),
    (1, 0, 1, ((0, 2, 0), (3, 1, 0),)),
    (0, 1, 3, ()),
    (0, 2, 5, ()),
    (0, 3, 4, ()),
    (0, 2, 3, ()),
    (0, 0, 3, ()),
    (0, 2, 4, ()),
    (1, 0, 3, ()),
    (1, 1, 6, ((2, 6, 0), (3, 6, -1),)),
    (1, 2, 3, ()),
    (1, 2, 1, ()),
    (1, 1, 4, ((0, 4, 0), (1, 5, 0),)),
    (1, 2, 5, ((2, 4, 0),)),
    (1, 1, 2, ((2, 2, 0),)),
    (1, 0, 5, ((0, 6, 0),)),
    (1, 0, 2, ((3, 2, 0),)),
    (1, 3, 1, ()),
    (1, 3, 4, ()),
    (1, 2, 6, ()),
    (1, 3, 6, ()),
    (1, 0, 4, ()),
    (1, 1, 5, ()),
    (1, 2, 4, ()),
    (1, 2, 2, ()),
    (1, 3, 2, ()),
    (1, 0, 6, ()),
)

SLOT = {entry[:3]: i for i, entry in enumerate(TREE)}


def kernel(
    owner_ref, tile_ref, mblock_ref, coef_ref, t_hbm, out_ref,
    t_buf, c_buf0, c_buf1, rhs, acc, h_own, h_nbr, h_far, g_buf, g_nbr, z_out, z_in, y_sum, y_in,
    w_in, w_out, v_in, x_pad, x_out, x_in,
    t_sem, c_recv, c_send, cf_recv, cf_send, n_recv, n_send, f_recv, f_send, of_recv, of_send, nf_recv, nf_send,
    ff_recv, ff_send, z_recv, z_send, y_recv, y_send,
    w_recv, w_send, v_recv, v_send, x_recv, x_send,
):
    a, r = lax.axis_index("aux"), lax.axis_index("row")
    y, z = a // NZ, lax.rem(a, NZ)
    x, c = r // 2, lax.rem(r, 2)
    sign_z = 1 - 2 * c
    sign_y = sign_z * (1 - 2 * lax.rem(x, 2))

    def at(dx=0, dy=0, dz=0, flip=0):
        return {
            "aux": lax.rem(y + dy + NY, NY) * NZ + lax.rem(z + dz + NZ, NZ),
            "row": lax.rem(x + dx + NX, NX) * 2 + lax.rem(c + flip, 2),
        }

    def copy(src, dst, send, recv, device):
        return pltpu.make_async_remote_copy(
            src_ref=src, dst_ref=dst, send_sem=send, recv_sem=recv, device_id=device, device_id_type=MESH
        )

    c_bufs = (c_buf0, c_buf1)
    sibling = at(flip=1)
    t_copy = pltpu.make_async_copy(t_hbm, t_buf, t_sem)
    t_copy.start()
    partners = [sibling]
    partners += [at(dx=e) for e in (1, 3)]
    partners += [at(dy=e) for e in range(1, NY)]
    partners += [at(dz=e) for e in range(1, NZ)]
    mirrors = [{"aux": x * NZ + 4 * c + t, "row": y * 2 + z // 4} for t in range(4)]
    barrier = pltpu.get_barrier_semaphore()
    for device in partners:
        pl.semaphore_signal(barrier, inc=1, device_id=device, device_id_type=MESH)

    @pl.when(x != y)
    def _():
        for device in mirrors:
            pl.semaphore_signal(barrier, inc=1, device_id=device, device_id_type=MESH)

    for ch in range(2):
        for t in range(4):
            c_bufs[ch][a * 4 + t] = coef_ref[t * BLK:(t + 1) * BLK, ch * BLK:(ch + 1) * BLK]

    @pl.when(x == y)
    def _():
        pl.semaphore_wait(barrier, len(partners))

    @pl.when(x != y)
    def _():
        pl.semaphore_wait(barrier, len(partners) + len(mirrors))


    def relay(entry):
        ch, dy, dz, children = entry
        origin = lax.rem(y - sign_y * dy + NY, NY) * NZ + lax.rem(z - sign_z * dz + NZ, NZ)
        piece = c_bufs[ch].at[pl.ds(origin * 4 + 2 * c, 2)]
        if dy or dz:
            copy(piece, piece, c_send.at[ch], c_recv.at[SLOT[ch, dy, dz]], sibling).wait_recv()
        for child_dy, child_dz, dx in children:
            to = at(dx=dx) if dx else at(dy=sign_y * (child_dy - dy), dz=sign_z * (child_dz - dz))
            copy(piece, piece, c_send.at[ch], c_recv.at[SLOT[ch, child_dy, child_dz]], to).start()
        if dy or dz:
            copy(piece, piece, cf_send.at[ch], cf_recv.at[ch], sibling).start()

    carried = c_buf0.at[pl.ds(0, 62)]

    def wait_flipped(ch):
        copy(carried, carried, cf_send.at[ch], cf_recv.at[ch], sibling).wait_recv()

    def build_rhs(ch):
        for k in range(32):
            block = c_bufs[ch][owner_ref[k] * 4 + tile_ref[k]]
            zero = jnp.zeros_like(block)
            for b in range(2):
                rhs[k * BLK:(k + 1) * BLK, b * BLK:(b + 1) * BLK] = jnp.where(mblock_ref[k] == b, block, zero)

    def half_dot(g):
        lhs = jnp.concatenate([t_buf[:, 4 * g + j].reshape(8 * BLK, BLK) for j in range(4)], axis=1)
        product = jnp.dot(lhs, rhs[g * 512:(g + 1) * 512, :], preferred_element_type=F32)
        if g == 0:
            acc[...] = product
        else:
            acc[...] += product

    def store_half(ch):
        for p in range(8):
            for b in range(2):
                h_own[ch, c, p // 2, b * BLK:(b + 1) * BLK, p % 2 * BLK:(p % 2 + 1) * BLK] = acc[
                    p * BLK:(p + 1) * BLK, b * BLK:(b + 1) * BLK
                ].astype(BF16)

    def send_nbr(ch, side):
        return copy(
            h_own.at[ch, c, pl.ds(2 * side, 2)], h_nbr.at[ch, side, c], n_send.at[ch, side], n_recv.at[ch, side],
            at(dx=1 if side else 3),
        )

    def send_far(ch, side):
        to = lax.rem(x + (1 if side else 3), NX)
        return copy(
            h_nbr.at[ch, side, c, to // 2], h_far.at[ch, side, c], f_send.at[ch, side], f_recv.at[ch, side],
            at(dx=1 if side else 3),
        )

    def flip_own(ch):
        ref = h_own.at[ch, c]
        return copy(ref, ref, of_send.at[ch], of_recv.at[ch], sibling)

    def flip_nbr(ch, side):
        ref = h_nbr.at[ch, side, c]
        return copy(ref, ref, nf_send.at[ch, side], nf_recv.at[ch, side], sibling)

    def flip_far(ch, side):
        ref = h_far.at[ch, side, c]
        return copy(ref, ref, ff_send.at[ch, side], ff_recv.at[ch, side], sibling)

    def gram(d, src):
        total = None
        for ch in range(2):
            if d == 0:
                terms = [(h_own[ch, src, q], h_own[ch, c, q]) for q in range(4)]
            elif d == 2:
                terms = [(h_far[ch, j, src], h_own[ch, c, 2 * j + x // 2]) for j in range(2)]
            else:
                side = d // 2
                terms = [(h_nbr[ch, side, src, j], h_own[ch, c, 2 * side + j]) for j in range(2)]
            for rows, columns in terms:
                part = lax.dot_general(rows, columns, (((1,), (1,)), ((), ())), preferred_element_type=F32)
                total = part if total is None else total + part
        rows = pl.ds(pl.multiple_of(src * 256, 256), 256)
        if d % 2:
            g_nbr[d // 2, rows, :] = total
        else:
            g_buf[rows, :] = total
        z_out[d, rows, :] = total.astype(BF16)

    cores = (c, lax.rem(c + 1, 2))
    own_rows = pl.ds(pl.multiple_of(z * 64, 64), 64)

    def z_start(d, src):
        for t in range(4):
            to = 4 * src + t
            rows = pl.ds(pl.multiple_of(to * 64, 64), 64)
            send = copy(
                z_out.at[d, rows], z_in.at[d, lax.rem(to - z + 2 * NZ - 1, NZ)], z_send.at[d], z_recv.at[d],
                {"aux": y * NZ + to, "row": r},
            )
            pl.when(to != z)(send.start)

    def w_copy(d, rows):
        plane = lax.rem(x + d, NX)
        slot = lax.rem(y - plane + 2 * NY - 1, NY)
        to = {"aux": plane * NZ + z, "row": r}
        return plane, copy(z_out.at[d, rows], w_in.at[slot, rows], w_send.at[d // 2], w_recv.at[slot], to)

    def w_start(d, src):
        plane, send = w_copy(d, pl.ds(pl.multiple_of(src * 256, 256), 256))
        pl.when(plane != y)(send.start)

    def v_copy(e):
        rows = pl.ds(pl.multiple_of(lax.rem(z + e, NZ) * 64, 64), 64)
        return copy(w_out.at[rows], v_in.at[e - 1], v_send, v_recv, at(dz=e))

    near = lax.rem(x + y, 2) == 1

    def w_finish():
        for slot in range(NY - 1):
            copy(w_in.at[slot], w_in.at[slot], w_send.at[0], w_recv.at[slot], sibling).wait_recv()
        total = g_nbr[lax.rem(y - x + NY, NY) // 2]
        for slot in range(NY - 1):
            total = total + w_in[slot].astype(F32)
        w_out[...] = total.astype(BF16)
        g_nbr[0] = total
        for e in (4, 3, 5, 2, 6, 1, 7):
            v_copy(e).start()
        y_sum[1] = g_nbr[0, own_rows, :]

    def v_finish():
        copy(v_in, v_in, v_send, v_recv, sibling).wait_recv()
        total = y_sum[1]
        for e in range(NZ - 1):
            total = total + v_in[e].astype(F32)
        out_ref[...] = total

    def y_finish():
        for slot in range(NY - 1):
            copy(y_in.at[slot], y_in.at[slot], y_send.at[0], y_recv.at[slot], sibling).wait_recv()
        out_ref[...] = y_sum[lax.rem(y - x + NY, NY)] + y_in[0] + y_in[1] + y_in[2]

    def y_copy(d):
        plane = lax.rem(x + d, NX)
        slot = lax.rem(y - plane + 2 * NY - 1, NY)
        to = {"aux": plane * NZ + z, "row": r}
        return plane, copy(y_sum.at[d], y_in.at[slot], y_send.at[d], y_recv.at[slot], to)

    def z_finish(d):
        copy(z_in.at[d, pl.ds(0, 7)], z_in.at[d, pl.ds(0, 7)], z_send.at[d], z_recv.at[d], sibling).wait_recv()
        total = y_sum[d]
        for e in range(NZ - 1):
            total = total + z_in[d, e].astype(F32)
        y_sum[d] = total
        plane, send = y_copy(d)
        pl.when(plane != y)(send.start)

    done = max(i for i, entry in enumerate(TREE) if entry[0] == 0) + 1
    for entry in TREE[:done]:
        relay(entry)
    later = list(TREE[done:])
    wait_flipped(0)
    t_copy.wait()
    build_rhs(0)
    for g in range(8):
        half_dot(g)
        for _ in range(2):
            if later:
                relay(later.pop(0))
    store_half(0)
    for side in range(2):
        send_nbr(0, side).start()
    flip_own(0).start()
    for entry in later:
        relay(entry)
    wait_flipped(1)
    build_rhs(1)
    for g in range(8):
        half_dot(g)
    store_half(1)
    for side in range(2):
        send_nbr(1, side).start()
    flip_own(1).start()
    for ch in range(2):
        for side in range(2):
            send_nbr(ch, side).wait_recv()
            flip_nbr(ch, side).start()
            send_far(ch, side).start()
        if ch == 0:
            for own in range(2):
                flip_own(own).wait_recv()
            for src in range(2):
                gram(0, src)
                z_start(0, src)
            y_sum[0] = g_buf[own_rows, :]
    for side in range(2):
        gram(2 * side + 1, cores[0])
        w_start(2 * side + 1, cores[0])
    for side in range(2):
        for ch in range(2):
            flip_nbr(ch, side).wait_recv()
        gram(2 * side + 1, cores[1])
        w_start(2 * side + 1, cores[1])
    z_finish(0)
    for ch in range(2):
        for side in range(2):
            send_far(ch, side).wait_recv()
            flip_far(ch, side).start()
    gram(2, cores[0])
    z_start(2, cores[0])
    for ch in range(2):
        for side in range(2):
            flip_far(ch, side).wait_recv()
    gram(2, cores[1])
    z_start(2, cores[1])
    y_sum[2] = g_buf[own_rows, :]
    pl.when(near)(w_finish)
    z_finish(2)
    pl.when(near)(v_finish)
    pl.when(jnp.logical_not(near))(y_finish)

    def mirror_copy(t):
        return copy(x_out.at[pl.ds(t * 64, 64)], x_in.at[lax.rem(z, 4)], x_send, x_recv, mirrors[t])

    @pl.when(x != y)
    def _():
        x_pad[...] = jnp.zeros_like(x_pad)
        x_pad[pl.ds(pl.multiple_of(lax.rem(z, 2) * 64, 64), 64), :] = out_ref[...]
        x_out[...] = x_pad[...].T
        for t in range(4):
            mirror_copy(t).start()
        copy(x_in, x_in, x_send, x_recv, sibling).wait_recv()
        out_ref[:, 0:BLK] += x_in[0] + x_in[1]
        out_ref[:, BLK:2 * BLK] += x_in[2] + x_in[3]
        copy(x_in, x_in, x_send, x_recv, sibling).wait_send()

    for ch in range(2):
        copy(carried, carried, c_send.at[ch], c_recv.at[0], sibling).wait_send()
        copy(carried, carried, cf_send.at[ch], cf_recv.at[ch], sibling).wait_send()
        flip_own(ch).wait_send()
        for side in range(2):
            send_nbr(ch, side).wait_send()
            send_far(ch, side).wait_send()
            flip_nbr(ch, side).wait_send()
            flip_far(ch, side).wait_send()
    for d in (0, 2):
        copy(z_in.at[d, pl.ds(0, 7)], z_in.at[d, pl.ds(0, 7)], z_send.at[d], z_recv.at[d], sibling).wait_send()
        plane, send = y_copy(d)
        pl.when(plane != y)(send.wait_send)
    for d in (1, 3):
        plane, send = w_copy(d, pl.ds(0, 512))
        pl.when(plane != y)(send.wait_send)
    pl.when(near)(copy(v_in, v_in, v_send, v_recv, sibling).wait_send)


def shards(three_index, coeffs, pair_owner, pair_tile, pair_mblock):
    smem, vmem = pl.BlockSpec(memory_space=pltpu.SMEM), pl.BlockSpec(memory_space=pltpu.VMEM)
    dma = pltpu.SemaphoreType.DMA
    return pl.pallas_call(
        kernel,
        out_shape=jax.ShapeDtypeStruct((64, 256), F32),
        in_specs=[smem, smem, smem, vmem, pl.BlockSpec(memory_space=pl.ANY)],
        out_specs=vmem,
        scratch_shapes=[
            pltpu.VMEM((8, 32, BLK, BLK), BF16),
            pltpu.VMEM((128, BLK, BLK), BF16),
            pltpu.VMEM((128, BLK, BLK), BF16),
            pltpu.VMEM((32 * BLK, 256), BF16),
            pltpu.VMEM((8 * BLK, 256), F32),
            pltpu.VMEM((2, 2, 4, 256, 256), BF16),
            pltpu.VMEM((2, 2, 2, 2, 256, 256), BF16),
            pltpu.VMEM((2, 2, 2, 256, 256), BF16),
            pltpu.VMEM((512, 256), F32),
            pltpu.VMEM((2, 512, 256), F32),
            pltpu.VMEM((4, 512, 256), BF16),
            pltpu.VMEM((4, 8, 64, 256), BF16),
            pltpu.VMEM((4, 64, 256), F32),
            pltpu.VMEM((4, 64, 256), F32),
            pltpu.VMEM((4, 512, 256), BF16),
            pltpu.VMEM((512, 256), BF16),
            pltpu.VMEM((7, 64, 256), BF16),
            pltpu.VMEM((BLK, 256), F32),
            pltpu.VMEM((256, BLK), F32),
            pltpu.VMEM((4, 64, BLK), F32),
            dma, dma((64,)), dma((2,)), dma((2,)), dma((2,)),
            dma((2, 2)), dma((2, 2)), dma((2, 2)), dma((2, 2)), dma((2,)), dma((2,)),
            dma((2, 2)), dma((2, 2)), dma((2, 2)), dma((2, 2)),
            dma((4,)), dma((4,)), dma((4,)), dma((4,)),
            dma((4,)), dma((2,)), dma, dma, dma, dma,
        ],
        compiler_params=pltpu.CompilerParams(
            collective_id=0, has_side_effects=True, vmem_limit_bytes=56 * 1024 * 1024
        ),
        name="exchange",
    )(pair_owner.reshape(32), pair_tile.reshape(32), pair_mblock.reshape(32), coeffs, three_index)


def solution(mesh):
    placed = (
        P("aux", "row", None, None),
        P("aux", None),
        P("aux", "row", None),
        P("aux", "row"),
        P("aux", "row"),
    )
    return jax.shard_map(
        shards, mesh=mesh, in_specs=placed, out_specs=P("aux", "row"), check_vma=False
    )
```
